512 devices in a mesh: dp: 64 (over x, y_lo, z), ctx: 8 (over y_hi, core).
Axes of the slice: x: 4, y: 8 (y_hi: 4, y_lo: 2; y = y_hi * 2 + y_lo), z: 8, core: 2. Of those that a mesh axis runs over, the one named last changes fastest.
Arguments:
- query_in: bfloat16 [64, 1024, 1024], P('dp', 'ctx'), may hold values from -6 to 6
- key_in: bfloat16 [64, 1024, 1024], P('dp', 'ctx'), may hold values from -6 to 6
- value_in: bfloat16 [64, 1024, 1024], P('dp', 'ctx'), may hold values from -6 to 6
- gate_in: bfloat16 [64, 1024, 1024], P('dp', 'ctx'), may hold values from -6 to 6
- out_grad: bfloat16 [64, 1024, 1024], P('dp', 'ctx'), may hold values from -6 to 6
- out_weight: bfloat16 [1024, 1024], P('dp'), may hold values from -0.1875 to 0.1875
- lengths: int32 [64, 8], P('dp'), may hold values from 1 to 512, 1024 in all within a row
- stamps: int32 [64, 1024], P('dp'), may hold values from 1 to 6291456, as said below
- pos_bias: float32 [1024], replicated, may hold values from -3 to 3
- time_bias: float32 [32], replicated, may hold values from -3 to 3
Outputs:
- layer_out: bfloat16 [64, 1024, 1024], P('dp', 'ctx')
- query_grad: bfloat16 [64, 1024, 1024], P('dp', 'ctx')
- key_grad: bfloat16 [64, 1024, 1024], P('dp', 'ctx')
- value_grad: bfloat16 [64, 1024, 1024], P('dp', 'ctx')
- gate_grad: bfloat16 [64, 1024, 1024], P('dp', 'ctx')
- weight_grad: float32 [1024, 1024], P('dp')
- pos_grad: float32 [1024], replicated
- time_grad: float32 [32], replicated
The draws below stay inside these ranges and needn't reach their ends.
Inputs may be any that keep to these rules, and one draw needn't show every extreme that they name: In every pack the 8 lengths add up to 1024 and the longest is exactly 512. `stamps`: timestamps rise strictly along each pack; each pack's first is 1 and its last is 6291456.
All inputs are finite; a program needn't handle non-finite values.
Results may differ from the reference program's by a relative error of at most 0.015.
Values may be sent and summed in bfloat16 or wider, within the bound.
A program may use at most 64 MiB of HBM per device.

```python
import math
import jax
import jax.numpy as jnp
import numpy as np
from jax import lax

HEADS = 8
HEAD_DIM = 128
D = 1024
USERS = 8
TIME_BUCKETS = 32
CONTEXT = 1024
PACKS = 64


def draw_stamps(key, part):
    key = jax.random.fold_in(key, 11)
    key_power, key_scale = jax.random.split(key)
    exponent = jax.random.randint(key_power, (PACKS, CONTEXT), 0, 12)
    multiple = jax.random.randint(key_scale, (PACKS, CONTEXT), 1, 4)
    step_gaps = jnp.left_shift(multiple, exponent).astype(jnp.int32)
    columns = lax.broadcasted_iota(jnp.int32, (PACKS, CONTEXT), 1)
    step_gaps = jnp.where(columns == 0, 1, step_gaps).astype(jnp.int32)
    inner = jnp.where(columns == CONTEXT - 1, 0, step_gaps).astype(jnp.int32)
    inner_total = jnp.sum(inner, axis=1, keepdims=True).astype(jnp.int32)
    closing = (CONTEXT * 6144 - inner_total).astype(jnp.int32)
    step_gaps = jnp.where(columns == CONTEXT - 1, closing, inner).astype(jnp.int32)
    return jnp.cumsum(step_gaps, axis=1).astype(jnp.int32)


def block_scale(key, extent, cuts, least, top_value):
    gain, own = 1.0, jax.random.fold_in(key, 6)
    for axis_at, parts in cuts:
        heights = jnp.exp(jax.random.uniform(jax.random.fold_in(own, axis_at), (parts,), jnp.float32, least / len(cuts), top_value / len(cuts)))
        gain = gain * jnp.repeat(heights, extent[axis_at] // parts).reshape([-1 if axis == axis_at else 1 for axis in range(len(extent))])
    return gain


def profile(number_of, total, most, slope):
    weights = [(1 << 20) // math.isqrt(standing ** slope) + 1 for standing in range(2, number_of + 1)]
    surplus, holding = total - most - (number_of - 1), [1] * (number_of - 1)
    while surplus > 0:
        candidates = [i for i in range(number_of - 1) if holding[i] < most]
        pool, left = sum([weights[i] for i in candidates]), surplus
        for i in candidates:
            more = min(most - holding[i], max(1, left * weights[i] // pool), surplus)
            holding[i] = holding[i] + more
            surplus = surplus - more
    return np.array([most] + holding)


def uneven_parts(own_key, amount, total, reach, skew):
    if amount == 2:
        one = jax.random.randint(own_key, (), max(1, total - reach), min(reach, total - 1) + 1)
        return jnp.stack([one, total - one])
    sizes = jnp.asarray(profile(amount, total, reach, skew), jnp.int32)
    twos = (amount - 1) // 2
    donor, taker = sizes[1:1 + 2 * twos:2], sizes[2:2 + 2 * twos:2]
    margin = jnp.minimum(donor - 1, reach - taker)
    passed = jax.random.randint(jax.random.fold_in(own_key, 1), (twos,), 0, 1 << 20) % (margin + 1)
    sizes = sizes.at[1:1 + 2 * twos:2].set(donor - passed).at[2:2 + 2 * twos:2].set(taker + passed)
    return sizes[jax.random.permutation(jax.random.fold_in(own_key, 2), amount)]


def scatter_about(key, dims, scale, bound, pieces=(), held_as=jnp.bfloat16):
    level = block_scale(key, dims, pieces, -0.22, 0.18) if pieces else 1.0
    drawn = jax.random.normal(key, dims, jnp.float32) * scale * level
    return jnp.minimum(jnp.maximum(drawn, -bound), bound).astype(held_as)


def setup_inputs(seed: int = 0) -> dict:
    splits = jax.random.split(jax.random.key(seed), 11)
    return {
        "query_in": scatter_about(splits[0], (PACKS, CONTEXT, D), 1.0, 6.0, ((0, 64), (1, 8))),
        "key_in": scatter_about(splits[1], (PACKS, CONTEXT, D), 1.0, 6.0, ((0, 64), (1, 8))),
        "value_in": scatter_about(splits[2], (PACKS, CONTEXT, D), 1.0, 6.0, ((0, 64), (1, 8))),
        "gate_in": scatter_about(splits[3], (PACKS, CONTEXT, D), 1.0, 6.0, ((0, 64), (1, 8))),
        "out_grad": scatter_about(splits[4], (PACKS, CONTEXT, D), 1.0, 6.0, ((0, 64), (1, 8))),
        "out_weight": scatter_about(splits[5], (D, D), D ** -0.5, 0.1875, ((0, 64),)),
        "lengths": jax.vmap(lambda own: uneven_parts(own, USERS, CONTEXT, CONTEXT // 2, 2))(jax.random.split(splits[6], PACKS)).reshape((PACKS, USERS)).astype(jnp.int32),
        "stamps": draw_stamps(jax.random.fold_in(splits[10], 71), 0),
        "pos_bias": scatter_about(splits[8], (CONTEXT,), 0.5, 3.0, (), jnp.float32),
        "time_bias": scatter_about(splits[9], (TIME_BUCKETS,), 0.5, 3.0, (), jnp.float32),
    }


EPSILON = 1e-06

def bucket_of(time_gap):
    bucket = jnp.zeros(time_gap.shape, jnp.int32)
    for shift_by in range(31):
        bucket = bucket + (time_gap >= 1 << shift_by).astype(jnp.int32)
    return bucket

def as_float(tensor):
    return tensor.astype(jnp.float32)

def head_view(tensor):
    return as_float(tensor).reshape(CONTEXT, HEADS, HEAD_DIM)

def one_pack(out_weight, pos_bias, time_bias, query_in, key_in, value_in, gate_in, out_grad, lengths, stamps):
    places = lax.iota(jnp.int32, CONTEXT)
    user_ends = jnp.cumsum(lengths).astype(jnp.int32)
    user_ids = lax.optimization_barrier(jnp.sum((places[:, None] >= user_ends[None, :]).astype(jnp.int32), axis=1))
    pair_mask = (user_ids[:, None] == user_ids[None, :]) & (places[:, None] >= places[None, :])
    relative = jnp.clip(places[:, None] - places[None, :], 0, CONTEXT - 1).astype(jnp.int32)
    bucket = bucket_of(jnp.abs(stamps[:, None] - stamps[None, :]))

    def bias_of(table_pos, table_time):
        return table_pos[relative] + table_time[bucket]
    pair_bias, pull_back = jax.vjp(bias_of, pos_bias, time_bias)
    factor = HEAD_DIM ** (-0.5)
    highest = lax.Precision.HIGHEST
    query_heads = head_view(query_in)
    key_heads = head_view(key_in)
    value_heads = head_view(value_in)
    scores = jnp.einsum('rhd,chd->hrc', query_heads, key_heads, precision=highest) * factor + pair_bias[None]
    weights = jnp.where(pair_mask[None], jax.nn.silu(scores), 0.0).astype(jnp.bfloat16)
    weights_wide = as_float(lax.optimization_barrier(weights))
    attended = jnp.einsum('hrc,chd->rhd', weights_wide, value_heads, precision=highest).reshape(CONTEXT, D).astype(jnp.bfloat16)
    attended_wide = as_float(attended)
    center = attended_wide - lax.optimization_barrier(jnp.mean(attended_wide, axis=1, keepdims=True))
    inv_dev = lax.rsqrt(lax.optimization_barrier(jnp.mean(center * center, axis=1, keepdims=True)) + EPSILON)
    normed = center * inv_dev
    mixed_rows = (normed * as_float(gate_in)).astype(jnp.bfloat16)
    layer_out = jnp.dot(mixed_rows, out_weight, preferred_element_type=jnp.float32).astype(jnp.bfloat16)
    mixed_grad = jnp.dot(out_grad, out_weight.T, preferred_element_type=jnp.float32)
    gate_grad = (mixed_grad * normed).astype(jnp.bfloat16)
    normed_grad = mixed_grad * as_float(gate_in)
    attn_grad = inv_dev * (normed_grad - lax.optimization_barrier(jnp.mean(normed_grad, axis=1, keepdims=True)) - normed * lax.optimization_barrier(jnp.mean(normed_grad * normed, axis=1, keepdims=True)))
    attn_grad = attn_grad.astype(jnp.bfloat16)
    weight_term = jnp.dot(mixed_rows.T, out_grad, preferred_element_type=jnp.float32)
    grad_heads = head_view(attn_grad)
    weight_grads = jnp.einsum('rhd,chd->hrc', grad_heads, value_heads, precision=highest)
    gate_sig = jax.nn.sigmoid(scores)
    score_grad = jnp.where(pair_mask[None], weight_grads * gate_sig * (1.0 + scores * (1.0 - gate_sig)), 0.0)
    pos_part, time_part = pull_back(lax.optimization_barrier(jnp.sum(score_grad, axis=0)))
    score_narrow = as_float(lax.optimization_barrier(score_grad.astype(jnp.bfloat16)))
    query_grad = (factor * jnp.einsum('hrc,chd->rhd', score_narrow, key_heads, precision=highest)).reshape(CONTEXT, D)
    key_grad = (factor * jnp.einsum('hrc,rhd->chd', score_narrow, query_heads, precision=highest)).reshape(CONTEXT, D)
    value_grad = jnp.einsum('hrc,rhd->chd', weights_wide, grad_heads, precision=highest).reshape(CONTEXT, D)
    rows_out = (layer_out, query_grad.astype(jnp.bfloat16), key_grad.astype(jnp.bfloat16), value_grad.astype(jnp.bfloat16), gate_grad)
    return (rows_out, (weight_term, pos_part, time_part))

def reference(query_in, key_in, value_in, gate_in, out_grad, out_weight, lengths, stamps, pos_bias, time_bias):

    def step_pack(sums, pack):
        rows_out, terms = one_pack(out_weight, pos_bias, time_bias, pack[0], pack[1], pack[2], pack[3], pack[4], pack[5], pack[6])
        return ((sums[0] + terms[0], sums[1] + terms[1], sums[2] + terms[2]), rows_out)
    start_sums = (jnp.zeros((D, D), jnp.float32), jnp.zeros((CONTEXT,), jnp.float32), jnp.zeros((TIME_BUCKETS,), jnp.float32))
    sums, stacked = lax.scan(step_pack, start_sums, (query_in, key_in, value_in, gate_in, out_grad, lengths, stamps))
    return (stacked[0], stacked[1], stacked[2], stacked[3], stacked[4], sums[0], sums[1], sums[2])
```

```python
import functools

import jax
import jax.numpy as jnp
from jax import lax
from jax.experimental import pallas as pl
from jax.experimental.pallas import tpu as pltpu
from jax.sharding import PartitionSpec as P

HEAD = 128
ROWS = 128
CTX = 8
COLS = 1024
PAD = 512
SLAB = PAD + ROWS
NX, NYL, NZ, NYH = 4, 2, 8, 4
WROWS = 16
EPSILON = 1e-06
FACTOR = HEAD ** (-0.5)
MASKED = -1e30
BUCKETS = 24
F32 = jnp.float32
BF16 = jnp.bfloat16
NT = (((1,), (1,)), ((), ()))


def dot(a, b):
    return jnp.dot(a, b, preferred_element_type=F32)


def dot_nt(a, b):
    return lax.dot_general(a, b, NT, preferred_element_type=F32)


def aligned(start, size=128):
    return pl.multiple_of(start, size)


def lanes_reversed(block):
    lane = lax.broadcasted_iota(jnp.int32, block.shape, 1)
    return jnp.take_along_axis(block, 127 - lane, axis=1, mode="promise_in_bounds")


def gate_of(scores):
    return 0.5 * jnp.tanh(0.5 * scores) + 0.5


def kernel(
    q_in, k_in, v_in, g_in, og_in, w_in, len_ref, stamp_ref, pos_ref, time_ref,
    lo_out, dq_out, dk_out, dv_out, gg_out, wg_out, pos_out, time_out,
    qh, kh, vh, doh, o_send, o_row, a_send, gate, ograd, mixed, mgrad, wbuf,
    stamp_pad, tz, bias, bucket, wts, wts_t, q_t, dk_t, dv_sum, d_send, pos_fold,
    lo_v, gg_v, w_send, w_own, w_r0, w_s0, w_r1, w_s1, w_r2, w_s2, w_r3, w_s3, w_land,
    b_v, b_r,
    loc, qkv_s, qkv_r, wz_s, wz_r, wx_s, wx_r, wy_s, wy_r, wc_s, wc_r,
    o_s, o_r, a_s, a_r, d_s, d_r, rc_s, rc_r, rx_s, rx_r, rz_s, rz_r, ry_s, ry_r,
    ag_s, ag_r, b_s, b_rs,
):
    dp = lax.axis_index("dp")
    me = lax.axis_index("ctx")
    z = lax.rem(dp, NZ)
    yl = lax.rem(lax.div(dp, NZ), NYL)
    x = lax.div(dp, NZ * NYL)
    core = lax.rem(me, 2)
    yh = lax.div(me, 2)

    def dp_of(xx, yy, zz):
        return (xx * NYL + yy) * NZ + zz

    def ctx_peer(k):
        return (dp, lax.rem(me + k, CTX))

    def z_peer(k):
        return (dp_of(x, yl, lax.rem(z + k, NZ)), me)

    def x_peer(k):
        return (dp_of(lax.rem(x + k, NX), yl, z), me)

    def xy_peer(k):
        return (dp_of(lax.rem(x + k // 2, NX), lax.rem(yl + k % 2, NYL), z), me)

    def y_peer(k):
        return (dp_of(x, lax.rem(yl + k // NYH, NYL), z), lax.rem(yh + k % NYH, NYH) * 2 + core)

    def remote(src, dst, send_sem, recv_sem, where):
        return pltpu.make_async_remote_copy(
            src_ref=src,
            dst_ref=dst,
            send_sem=send_sem,
            recv_sem=recv_sem,
            device_id=where,
            device_id_type=pl.DeviceIdType.MESH,
        )

    partners = [ctx_peer(k) for k in range(1, CTX)]
    partners += [z_peer(k) for k in range(1, NZ)]
    partners += [xy_peer(k) for k in range(1, NX * NYL)]
    partners += [y_peer(NYH + k) for k in range(1, NYH)]
    barrier = pltpu.get_barrier_semaphore()
    for where in partners:
        pl.semaphore_signal(barrier, inc=1, device_id=where, device_id_type=pl.DeviceIdType.MESH)

    my_rows = pl.ds(aligned(me * ROWS), ROWS)
    my_pad_rows = pl.ds(aligned(PAD + me * ROWS), ROWS)
    my_cols = pl.ds(aligned(me * HEAD), HEAD)
    half = pl.ds(aligned(core * 512), 512)
    w_rows = pl.ds(aligned(z * WROWS, WROWS), WROWS)
    own_copies = [
        pltpu.make_async_copy(q_in.at[0, :, my_cols], qh.at[my_rows], loc.at[0]),
        pltpu.make_async_copy(k_in.at[0, :, my_cols], kh.at[my_pad_rows], loc.at[1]),
        pltpu.make_async_copy(v_in.at[0, :, my_cols], vh.at[my_pad_rows], loc.at[2]),
        pltpu.make_async_copy(g_in.at[0], gate, loc.at[3]),
        pltpu.make_async_copy(og_in.at[0], ograd, loc.at[4]),
        pltpu.make_async_copy(w_in.at[:, half], wbuf.at[x, yl, w_rows, half], loc.at[5]),
    ]
    for copy in own_copies:
        copy.start()

    kh[0:PAD, :] = jnp.zeros((PAD, HEAD), BF16)
    vh[0:PAD, :] = jnp.zeros((PAD, HEAD), BF16)
    stamp_pad[:, 0:PAD] = jnp.zeros((1, PAD), jnp.int32)
    stamp_pad[:, PAD:] = stamp_ref[...]

    reversed_pos = lanes_reversed(pos_ref[...])
    line = jnp.concatenate(
        [reversed_pos[4 - b : 5 - b, :] for b in range(5)] + [jnp.zeros((1, 128), F32)], axis=1
    )
    sheet = pltpu.roll(jnp.broadcast_to(line, (ROWS, 768)), 1, 1)
    row_no = lax.broadcasted_iota(jnp.int32, (ROWS, 768), 0)
    for bit in range(7):
        rolled = pltpu.roll(sheet, 1 << bit, 1)
        sheet = jnp.where((row_no & (1 << bit)) != 0, rolled, sheet)
    tz[...] = sheet[:, 128:]

    pl.semaphore_wait(barrier, len(partners))

    def qkv_copy(a, k):
        where = ctx_peer(k)
        cols = pl.ds(aligned(where[1] * HEAD), HEAD)
        src = (q_in, k_in, v_in)[a].at[0, :, cols]
        dst = (qh.at[my_rows], kh.at[my_pad_rows], vh.at[my_pad_rows])[a]
        return remote(src, dst, qkv_s.at[a, k], qkv_r.at[a, k], where)

    def wz_copy(k):
        return remote(w_in.at[:, half], wbuf.at[x, yl, w_rows, half], wz_s.at[k], wz_r.at[k], z_peer(k))

    for k in range(1, NZ):
        wz_copy(k).start()
    for a in (0, 1, 2):
        for k in (3, 4, 5, 2, 6, 1, 7):
            qkv_copy(a, k).start()

    r_iota = lax.broadcasted_iota(jnp.int32, (ROWS, 128), 0)
    c_iota = lax.broadcasted_iota(jnp.int32, (ROWS, 128), 1)
    table = jnp.zeros((ROWS, 128), F32)
    for b in range(32):
        table = jnp.where(c_iota == b, time_ref[b], table)
    starts = []
    total = jnp.int32(0)
    for u in range(8):
        starts.append(total)
        total = total + len_ref[0, u]

    def bias_slab(i, unused):
        row_stamps = stamp_pad[:, pl.ds(aligned(PAD + i * ROWS), ROWS)]
        stamp_col = jnp.transpose(jnp.broadcast_to(row_stamps, (ROWS, 128)))
        place = r_iota + i * ROWS
        start = jnp.zeros((ROWS, 128), jnp.int32)
        for u in range(1, 8):
            start = jnp.where(place >= starts[u], jnp.maximum(start, starts[u]), start)
        first_col = start - (i * ROWS - PAD)
        for b in range(5):
            key_stamps = stamp_pad[:, pl.ds(aligned(i * ROWS + b * 128), 128)]
            gap = stamp_col - key_stamps
            number = 32 - lax.clz(gap)
            timed = jnp.take_along_axis(table, number, axis=1, mode="promise_in_bounds")
            col = c_iota + b * 128
            mask = (col >= first_col) & (col <= r_iota + PAD)
            cols = slice(b * 128, b * 128 + 128)
            bias[i, :, cols] = jnp.where(mask, tz[:, cols] + timed, MASKED)
            bucket[i, :, cols] = number
        return unused

    lax.fori_loop(0, CTX, bias_slab, 0)

    def wx_copy(k):
        mine = wbuf.at[x, yl, :, half]
        return remote(mine, mine, wx_s.at[k], wx_r.at[k], x_peer(k))

    own_copies[5].wait()
    for k in range(1, NZ):
        wz_copy(k).wait_recv()
    for k in range(1, NX):
        wx_copy(k).start()

    for copy in own_copies[:5]:
        copy.wait()
    for a in (0, 1, 2):
        for k in range(1, CTX):
            qkv_copy(a, k).wait_recv()

    def forward(i):
        rows = pl.ds(aligned(i * ROWS), ROWS)
        slab = pl.ds(aligned(i * ROWS), SLAB)
        pair_bias = bias[i]
        scores = dot_nt(qh[rows, :], kh[slab, :]) * FACTOR + pair_bias
        weights = jnp.where(pair_bias > 0.1 * MASKED, scores * gate_of(scores), 0.0).astype(BF16)
        bias[i] = scores
        wts[i] = weights
        return dot(weights, vh[slab, :]).astype(BF16)

    def o_copy(k):
        where = ctx_peer(k)
        return remote(o_send.at[where[1]], o_row.at[:, my_cols], o_s.at[k], o_r.at[k], where)

    def forward_step(k, unused):
        i = lax.rem(me + k, CTX)
        o_send[i] = forward(i)
        o_copy(k).start()
        return unused

    lax.fori_loop(1, CTX, forward_step, 0)
    o_row[:, my_cols] = forward(me)

    def wy_copy(way):
        peer_yh = lax.rem(yh + yl + (0 if way == 0 else NYH - 1), NYH)
        part = wbuf.at[pl.ds(2 * way, 2), yl, :, half]
        where = (dp_of(x, 1 - yl, z), peer_yh * 2 + core)
        return remote(part, part, wy_s.at[way], wy_r.at[way], where)

    def wc_copy():
        part = wbuf.at[:, :, :, half]
        return remote(part, part, wc_s.at[0], wc_r.at[0], (dp, yh * 2 + 1 - core))

    for k in range(1, NX):
        wx_copy(k).wait_recv()
    for way in range(2):
        wy_copy(way).start()

    def prepare(i, unused):
        scores = bias[i]
        sig = gate_of(scores)
        slope = sig * (1.0 + scores * (1.0 - sig))
        bias[i] = jnp.where(scores > 0.1 * MASKED, slope, 0.0)
        rows = pl.ds(aligned(i * ROWS), ROWS)
        q_t[:, rows] = jnp.transpose(qh[rows, :])
        wts_t[i] = jnp.transpose(wts[i])
        return unused

    lax.fori_loop(0, CTX, prepare, 0)
    dk_t[...] = jnp.zeros(dk_t.shape, F32)
    dv_sum[...] = jnp.zeros(dv_sum.shape, F32)

    for way in range(2):
        wy_copy(way).wait_recv()
    wc_copy().start()
    wc_copy().wait_recv()

    def mixed_grad_part(n, unused):
        block = wbuf[n].reshape(256, COLS)
        mgrad[:, pl.ds(aligned(n * 256), 256)] = dot_nt(ograd[...], block)
        return unused

    lax.fori_loop(0, NX, mixed_grad_part, 0)

    for k in range(1, CTX):
        o_copy(k).wait_recv()

    def rows_part(n, unused):
        rows = pl.ds(aligned(n * 32, 32), 32)
        attended = o_row[rows, :].astype(F32)
        center = attended - jnp.mean(attended, axis=1, keepdims=True)
        inv_dev = lax.rsqrt(jnp.mean(center * center, axis=1, keepdims=True) + EPSILON)
        normed = center * inv_dev
        gate_wide = gate[rows, :].astype(F32)
        grad = mgrad[rows, :]
        mixed[rows, :] = (normed * gate_wide).astype(BF16)
        gg_v[rows, :] = (grad * normed).astype(BF16)
        normed_grad = grad * gate_wide
        first = jnp.mean(normed_grad, axis=1, keepdims=True)
        second = jnp.mean(normed_grad * normed, axis=1, keepdims=True)
        a_send[rows, :] = (inv_dev * (normed_grad - first - normed * second)).astype(BF16)
        return unused

    lax.fori_loop(0, 4, rows_part, 0)

    def a_copy(k):
        where = ctx_peer(k)
        cols = pl.ds(aligned(where[1] * HEAD), HEAD)
        return remote(a_send.at[:, cols], doh.at[my_rows], a_s.at[k], a_r.at[k], where)

    for k in range(1, CTX):
        a_copy(k).start()
    doh[my_rows, :] = a_send[:, my_cols]

    other_half = pl.ds(aligned((1 - core) * 512), 512)

    def rc_copy(k):
        part = lax.rem(x + k, NX)
        return remote(w_send.at[part], w_r0.at[part], rc_s.at[k], rc_r.at[k], (dp, yh * 2 + 1 - core))

    def weight_part(k, unused):
        part = lax.rem(x + k, NX)
        turned = jnp.transpose(mixed[:, pl.ds(aligned(part * 256), 256)])
        w_send[part] = dot(turned, ograd[:, other_half]).astype(BF16)
        rc_copy(k).start()
        w_own[part] = dot(turned, ograd[:, half])
        return unused

    lax.fori_loop(1, NX + 1, weight_part, 0)

    def layer_part(n, unused):
        cols = pl.ds(aligned(n * 256), 256)
        block = wbuf[:, :, :, cols].reshape(COLS, 256)
        lo_v[:, cols] = dot(mixed[...], block).astype(BF16)
        return unused

    lax.fori_loop(0, 4, layer_part, 0)
    out_copies = [
        pltpu.make_async_copy(lo_v, lo_out.at[0], loc.at[6]),
        pltpu.make_async_copy(gg_v, gg_out.at[0], loc.at[7]),
    ]
    for copy in out_copies:
        copy.start()

    def rx_copy(k):
        part = lax.rem(x + k, NX)
        return remote(w_s0.at[part], w_r1.at[k], rx_s.at[k], rx_r.at[k], x_peer(k))

    def core_sum(k, unused):
        part = lax.rem(x + k, NX)
        rc_copy(k).wait_recv()
        w_s0[part] = (w_own[part] + w_r0[part].astype(F32)).astype(BF16)
        rx_copy(k).start()
        return unused

    lax.fori_loop(1, NX, core_sum, 0)
    rc_copy(NX).wait_recv()

    for k in range(1, CTX):
        a_copy(k).wait_recv()

    def backward(i):
        rows = pl.ds(aligned(i * ROWS), ROWS)
        slab = pl.ds(aligned(i * ROWS), SLAB)
        grad = doh[rows, :]
        score_grad = dot_nt(grad, vh[slab, :]) * bias[i]
        bias[i] = score_grad
        narrow = score_grad.astype(BF16)
        dk_t[:, slab] += dot(q_t[:, rows], narrow)
        dv_sum[slab, :] += dot(wts_t[i], grad)
        return (dot(narrow, kh[slab, :]) * FACTOR).astype(BF16)

    outs = (dq_out, dk_out, dv_out)

    def d_copy(a, k):
        where = ctx_peer(k)
        return remote(d_send.at[a, where[1]], outs[a].at[0, :, my_cols], d_s.at[a, k], d_r.at[a, k], where)

    def backward_step(k, unused):
        i = lax.rem(me + k, CTX)
        d_send[0, i] = backward(i)
        d_copy(0, k).start()
        return unused

    lax.fori_loop(1, CTX, backward_step, 0)
    d_send[0, me] = backward(me)

    def key_value_block(i):
        rows = pl.ds(aligned(PAD + i * ROWS), ROWS)
        d_send[1, i] = (jnp.transpose(dk_t[:, rows]) * FACTOR).astype(BF16)
        d_send[2, i] = dv_sum[rows, :].astype(BF16)

    def key_value_step(k, unused):
        key_value_block(lax.rem(me + k, CTX))
        d_copy(1, k).start()
        d_copy(2, k).start()
        return unused

    lax.fori_loop(1, CTX, key_value_step, 0)
    key_value_block(me)
    d_own = [
        pltpu.make_async_copy(d_send.at[a, me], outs[a].at[0, :, my_cols], loc.at[8 + a])
        for a in range(3)
    ]
    for copy in d_own:
        copy.start()

    def rz_copy(k):
        rows = pl.ds(aligned(lax.rem(z + k, NZ) * WROWS, WROWS), WROWS)
        return remote(w_s1.at[:, rows], w_r2.at[k], rz_s.at[k], rz_r.at[k], z_peer(k))

    for k in range(1, NX):
        rx_copy(k).wait_recv()

    def x_sum(n, unused):
        rows = pl.ds(aligned(n * 32, 32), 32)
        total = w_own[x, rows, :] + w_r0[x, rows, :].astype(F32)
        for k in range(1, NX):
            total = total + w_r1[k, rows, :].astype(F32)
        w_s1[lax.div(n, 4), pl.ds(aligned(lax.rem(n, 4) * 32, 32), 32), :] = total.astype(BF16)
        return unused

    lax.fori_loop(0, 8, x_sum, 0)
    for k in range(1, NZ):
        rz_copy(k).start()

    pos_fold[:, 0:128] = jnp.zeros((ROWS, 128), F32)

    def slab_sum(n, unused):
        rows = pl.ds(aligned(n * 8, 8), 8)
        total = bias[0, rows, :]
        for i in range(1, CTX):
            total = total + bias[i, rows, :]
        pos_fold[rows, 128:] = total
        return unused

    lax.fori_loop(0, 16, slab_sum, 0)
    fold = pos_fold[...]
    for count in (64, 32, 16, 8):
        fold = fold[:count] + pltpu.roll(fold[count : 2 * count], 768 - count, 1)
    row_no = lax.broadcasted_iota(jnp.int32, (8, 768), 0)
    for count in (4, 2, 1):
        fold = jnp.where((row_no & count) != 0, pltpu.roll(fold, 768 - count, 1), fold)
    fold = pltpu.roll(fold, 767, 1)
    fold = jnp.broadcast_to(jnp.sum(fold, axis=0, keepdims=True), (8, 768))
    row8 = lax.broadcasted_iota(jnp.int32, (8, 128), 0)
    lane8 = lax.broadcasted_iota(jnp.int32, (8, 128), 1)
    sums = jnp.zeros((8, 128), F32)
    for b in range(4):
        block = lanes_reversed(fold[:, (4 - b) * 128 : (5 - b) * 128])
        sums = jnp.where(row8 == b, block, sums)

    def histogram(n, totals):
        i = lax.div(n, 16)
        rows = pl.ds(aligned(lax.rem(n, 16) * 8, 8), 8)
        grads = bias[i, rows, :]
        numbers = bucket[i, rows, :]
        out = []
        for b in range(BUCKETS):
            hit = jnp.where(numbers == b, grads, 0.0)
            part = totals[b]
            for at in range(5):
                part = part + hit[:, at * 128 : at * 128 + 128]
            out.append(part)
        return tuple(out)

    totals = lax.fori_loop(
        0, 128, histogram, tuple(jnp.zeros((8, 128), F32) for unused in range(BUCKETS))
    )
    timed = jnp.zeros((8, 128), F32)
    for b in range(BUCKETS):
        whole = jnp.sum(jnp.sum(totals[b], axis=0, keepdims=True), axis=1, keepdims=True)
        timed = jnp.where(lane8 == b, whole, timed)
    sums = jnp.where(row8 == 4, timed, sums)

    slots = (me, z, x * NYL + yl)
    b_peers = (ctx_peer, z_peer, xy_peer)

    def b_copy(level, k):
        return remote(b_v.at[level], b_r.at[level, slots[level]], b_s.at[level, k], b_rs.at[level, k], b_peers[level](k))

    def b_start(level, value):
        b_v[level] = value
        b_r[level, slots[level]] = value
        for k in range(1, 8):
            b_copy(level, k).start()

    def b_finish(level):
        for k in range(1, 8):
            b_copy(level, k).wait_recv()
        value = b_r[level, 0]
        for slot in range(1, 8):
            value = value + b_r[level, slot]
        return value

    b_start(0, sums)

    def ry_copy(k):
        to_yl = lax.rem(yl + k // NYH, NYL)
        cols = pl.ds(aligned(lax.rem(yh + k % NYH, NYH) * 128), 128)
        return remote(w_s2.at[to_yl, :, cols], w_r3.at[k], ry_s.at[k], ry_r.at[k], y_peer(k))

    for k in range(1, NZ):
        rz_copy(k).wait_recv()
    z_rows = pl.ds(aligned(z * WROWS, WROWS), WROWS)
    total = w_s1[:, z_rows, :].astype(F32)
    for k in range(1, NZ):
        total = total + w_r2[k].astype(F32)
    w_s2[...] = total
    for k in range(1, NYL * NYH):
        ry_copy(k).start()

    b_start(1, b_finish(0))

    for k in range(1, NYL * NYH):
        ry_copy(k).wait_recv()
    piece = w_s2[yl, :, pl.ds(aligned(yh * 128), 128)]
    for k in range(1, NYL * NYH):
        piece = piece + w_r3[k]
    w_s3[...] = piece
    piece_cols = pl.ds(aligned(core * 512 + yh * 128), 128)
    w_land[:, piece_cols] = piece

    def ag_copy(k):
        return remote(w_s3, w_land.at[:, piece_cols], ag_s.at[k], ag_r.at[k], ctx_peer(k))

    for k in range(1, CTX):
        ag_copy(k).start()

    b_start(2, b_finish(1))

    for k in range(1, CTX):
        ag_copy(k).wait_recv()
    wg_out[...] = w_land[...]

    sums = b_finish(2)
    pos_out[...] = jnp.where(row8 < 4, sums, 0.0)
    time_out[...] = jnp.broadcast_to(sums[4:5, :], (8, 128))

    for a in (0, 1, 2):
        for k in range(1, CTX):
            d_copy(a, k).wait_recv()
    for copy in d_own + out_copies:
        copy.wait()
    for k in range(1, CTX):
        for a in range(3):
            qkv_copy(a, k).wait_send()
            d_copy(a, k).wait_send()
            b_copy(a, k).wait_send()
        wz_copy(k).wait_send()
        o_copy(k).wait_send()
        a_copy(k).wait_send()
        rz_copy(k).wait_send()
        ry_copy(k).wait_send()
        ag_copy(k).wait_send()
    for k in range(1, NX):
        wx_copy(k).wait_send()
        rx_copy(k).wait_send()
    for k in range(1, NX + 1):
        rc_copy(k).wait_send()
    for way in range(2):
        wy_copy(way).wait_send()
    wc_copy().wait_send()


def on_device(
    query_in, key_in, value_in, gate_in, out_grad, out_weight, lengths, stamps, pos_bias, time_bias
):
    dma = lambda *shape: pltpu.SemaphoreType.DMA(shape)
    vmem = pltpu.VMEM
    anywhere = pl.BlockSpec(memory_space=pl.ANY)
    in_vmem = pl.BlockSpec(memory_space=pltpu.VMEM)
    in_smem = pl.BlockSpec(memory_space=pltpu.SMEM)
    rows_shape = jax.ShapeDtypeStruct((1, ROWS, COLS), BF16)
    outs = pl.pallas_call(
        kernel,
        out_shape=[rows_shape] * 5
        + [
            jax.ShapeDtypeStruct((WROWS, COLS), F32),
            jax.ShapeDtypeStruct((8, 128), F32),
            jax.ShapeDtypeStruct((8, 128), F32),
        ],
        in_specs=[anywhere] * 6 + [in_smem, in_vmem, in_vmem, in_smem],
        out_specs=[anywhere] * 5 + [in_vmem] * 3,
        scratch_shapes=[
            vmem((COLS, HEAD), BF16),
            vmem((PAD + COLS, HEAD), BF16),
            vmem((PAD + COLS, HEAD), BF16),
            vmem((COLS, HEAD), BF16),
            vmem((CTX, ROWS, HEAD), BF16),
            vmem((ROWS, COLS), BF16),
            vmem((ROWS, COLS), BF16),
            vmem((ROWS, COLS), BF16),
            vmem((ROWS, COLS), BF16),
            vmem((ROWS, COLS), BF16),
            vmem((ROWS, COLS), F32),
            vmem((NX, NYL, NZ * WROWS, COLS), BF16),
            vmem((1, PAD + COLS), jnp.int32),
            vmem((ROWS, SLAB), F32),
            vmem((CTX, ROWS, SLAB), F32),
            vmem((CTX, ROWS, SLAB), jnp.int32),
            vmem((CTX, ROWS, SLAB), BF16),
            vmem((CTX, SLAB, ROWS), BF16),
            vmem((HEAD, COLS), BF16),
            vmem((HEAD, PAD + COLS), F32),
            vmem((PAD + COLS, HEAD), F32),
            vmem((3, CTX, ROWS, HEAD), BF16),
            vmem((ROWS, 768), F32),
            vmem((ROWS, COLS), BF16),
            vmem((ROWS, COLS), BF16),
            vmem((NX, 256, 512), BF16),
            vmem((NX, 256, 512), F32),
            vmem((NX, 256, 512), BF16),
            vmem((NX, 256, 512), BF16),
            vmem((NX, 256, 512), BF16),
            vmem((NYL, 128, 512), BF16),
            vmem((NZ, NYL, WROWS, 512), BF16),
            vmem((NYL, WROWS, 512), F32),
            vmem((NYL * NYH, WROWS, 128), F32),
            vmem((WROWS, 128), F32),
            vmem((WROWS, COLS), F32),
            vmem((3, 8, 128), F32),
            vmem((3, 8, 8, 128), F32),
            dma(12),
            dma(3, 8), dma(3, 8),
            dma(8), dma(8),
            dma(4), dma(4),
            dma(2), dma(2),
            dma(1), dma(1),
            dma(8), dma(8),
            dma(8), dma(8),
            dma(3, 8), dma(3, 8),
            dma(5), dma(5),
            dma(4), dma(4),
            dma(8), dma(8),
            dma(8), dma(8),
            dma(8), dma(8),
            dma(3, 8), dma(3, 8),
        ],
        compiler_params=pltpu.CompilerParams(
            collective_id=0, has_side_effects=True, vmem_limit_bytes=56 * 1024 * 1024
        ),
    )(
        query_in,
        key_in,
        value_in,
        gate_in,
        out_grad,
        out_weight,
        lengths,
        stamps,
        pos_bias.reshape(8, 128),
        time_bias,
    )
    layer_out, query_grad, key_grad, value_grad, gate_grad, weight_grad, pos, timed = outs
    return (
        layer_out,
        query_grad,
        key_grad,
        value_grad,
        gate_grad,
        weight_grad,
        pos.reshape(COLS),
        timed[0, :32],
    )


def solution(mesh):
    rows = P("dp", "ctx", None)
    owned = P("dp", None)
    return jax.shard_map(
        on_device,
        mesh=mesh,
        in_specs=(rows, rows, rows, rows, rows, owned, owned, owned, P(), P()),
        out_specs=(rows, rows, rows, rows, rows, owned, P(), P()),
        check_vma=False,
    )
```

```python
import functools

import jax
import jax.numpy as jnp
from jax import lax
from jax.experimental import pallas as pl
from jax.experimental.pallas import tpu as pltpu
from jax.sharding import PartitionSpec as P

HEAD = 128
ROWS = 128
CTX = 8
COLS = 1024
PAD = 512
SLAB = PAD + ROWS
NX, NYL, NZ, NYH = 4, 2, 8, 4
WROWS = 16
EPSILON = 1e-06
FACTOR = HEAD ** (-0.5)
MASKED = -1e30
BUCKETS = 24
F32 = jnp.float32
BF16 = jnp.bfloat16
NT = (((1,), (1,)), ((), ()))


def dot(a, b):
    return jnp.dot(a, b, preferred_element_type=F32)


def dot_nt(a, b):
    return lax.dot_general(a, b, NT, preferred_element_type=F32)


def aligned(start, size=128):
    return pl.multiple_of(start, size)


def lanes_reversed(block):
    lane = lax.broadcasted_iota(jnp.int32, block.shape, 1)
    return jnp.take_along_axis(block, 127 - lane, axis=1, mode="promise_in_bounds")


def gate_of(scores):
    return 0.5 * jnp.tanh(0.5 * scores) + 0.5


def kernel(
    q_in, k_in, v_in, g_in, og_in, w_in, len_in, stamp_in, pos_in, time_in,
    lo_out, dq_out, dk_out, dv_out, gg_out, wg_out, pos_out, time_out,
    len_ref, stamp_ref, pos_ref, time_ref, table_v,
    qh, kh, vh, doh, o_send, o_row, a_send, gate, ograd, mixed, mgrad, wbuf,
    stamp_pad, tz, bias, bucket, wts, wts_t, q_t, dk_t, d_send, pos_fold,
    lo_v, gg_v, w_send, w_own, w_r0, w_s0, w_ax, w_a1, w_az, w_bz, w_b1, w_bx, w_s2, w_r3, w_s3, w_land,
    b_v, b_r,
    loc, qkv_s, qkv_r, wz_s, wz_r, wx_s, wx_r, wy_s, wy_r, wc_s, wc_r,
    o_s, o_r, a_s, a_r, d_s, d_r, rc_s, rc_r, rx_s, rx_r, rz_s, rz_r, ry_s, ry_r,
    ag_s, ag_r, b_s, b_rs,
):
    dp = lax.axis_index("dp")
    me = lax.axis_index("ctx")
    z = lax.rem(dp, NZ)
    yl = lax.rem(lax.div(dp, NZ), NYL)
    x = lax.div(dp, NZ * NYL)
    core = lax.rem(me, 2)
    yh = lax.div(me, 2)

    def dp_of(xx, yy, zz):
        return (xx * NYL + yy) * NZ + zz

    def ctx_peer(k):
        return (dp, lax.rem(me + k, CTX))

    def z_peer(k):
        return (dp_of(x, yl, lax.rem(z + k, NZ)), me)

    def x_peer(k):
        return (dp_of(lax.rem(x + k, NX), yl, z), me)

    def xy_peer(k):
        return (dp_of(lax.rem(x + k // 2, NX), lax.rem(yl + k % 2, NYL), z), me)

    def y_peer(k):
        return (dp_of(x, lax.rem(yl + k // NYH, NYL), z), lax.rem(yh + k % NYH, NYH) * 2 + core)

    def remote(src, dst, send_sem, recv_sem, where):
        return pltpu.make_async_remote_copy(
            src_ref=src,
            dst_ref=dst,
            send_sem=send_sem,
            recv_sem=recv_sem,
            device_id=where,
            device_id_type=pl.DeviceIdType.MESH,
        )

    partners = [ctx_peer(k) for k in range(1, CTX)]
    partners += [z_peer(k) for k in range(1, NZ)]
    partners += [xy_peer(k) for k in range(1, NX * NYL)]
    partners += [y_peer(NYH + k) for k in range(1, NYH)]
    barrier = pltpu.get_barrier_semaphore()
    for where in partners:
        pl.semaphore_signal(barrier, inc=1, device_id=where, device_id_type=pl.DeviceIdType.MESH)

    my_rows = pl.ds(aligned(me * ROWS), ROWS)
    my_pad_rows = pl.ds(aligned(PAD + me * ROWS), ROWS)
    my_cols = pl.ds(aligned(me * HEAD), HEAD)
    half = pl.ds(aligned(core * 512), 512)
    w_rows = pl.ds(aligned(z * WROWS, WROWS), WROWS)
    own_copies = [
        pltpu.make_async_copy(q_in.at[0, :, my_cols], qh.at[my_rows], loc.at[0]),
        pltpu.make_async_copy(k_in.at[0, :, my_cols], kh.at[my_pad_rows], loc.at[1]),
        pltpu.make_async_copy(v_in.at[0, :, my_cols], vh.at[my_pad_rows], loc.at[2]),
        pltpu.make_async_copy(g_in.at[0], gate, loc.at[3]),
        pltpu.make_async_copy(og_in.at[0], ograd, loc.at[4]),
        pltpu.make_async_copy(w_in.at[:, half], wbuf.at[x, yl, w_rows, half], loc.at[5]),
    ]
    small_copies = [
        pltpu.make_async_copy(len_in, len_ref, loc.at[11]),
        pltpu.make_async_copy(stamp_in, stamp_ref, loc.at[12]),
        pltpu.make_async_copy(pos_in, pos_ref, loc.at[13]),
        pltpu.make_async_copy(time_in, time_ref, loc.at[14]),
    ]
    for copy in small_copies:
        copy.start()
    pl.semaphore_wait(barrier, len(partners))

    def qkv_copy(a, k):
        where = ctx_peer(k)
        cols = pl.ds(aligned(where[1] * HEAD), HEAD)
        src = (q_in, k_in, v_in)[a].at[0, :, cols]
        dst = (qh.at[my_rows], kh.at[my_pad_rows], vh.at[my_pad_rows])[a]
        return remote(src, dst, qkv_s.at[a, k], qkv_r.at[a, k], where)

    def wy_copy():
        return remote(w_in.at[:, half], wbuf.at[x, yl, w_rows, half], wy_s.at[0], wy_r.at[0], (dp_of(x, 1 - yl, z), me))

    def wz_copy(which, k):
        dst = wbuf.at[x, yl if which == 0 else 1 - yl, w_rows, half]
        src = w_in.at[:, half] if which == 0 else dst
        return remote(src, dst, wz_s.at[which, k], wz_r.at[which, k], z_peer(k))

    def wx_copy(which, k):
        part = wbuf.at[x, yl if which == 0 else 1 - yl, :, half]
        return remote(part, part, wx_s.at[which, k], wx_r.at[which, k], x_peer(k))

    def wc_copy(k):
        part = wbuf.at[lax.rem(x + NX - k, NX), :, :, half]
        return remote(part, part, wc_s.at[k], wc_r.at[k], (dp, yh * 2 + 1 - core))

    wy_copy().start()
    for k in range(1, NZ):
        wz_copy(0, k).start()
    for k in (3, 4, 5, 2, 6, 1, 7):
        qkv_copy(0, k).start()
        qkv_copy(1, k).start()
    for copy in own_copies:
        copy.start()
    for k in (3, 4, 5, 2, 6, 1, 7):
        qkv_copy(2, k).start()

    kh[0:PAD, :] = jnp.zeros((PAD, HEAD), BF16)
    vh[0:PAD, :] = jnp.zeros((PAD, HEAD), BF16)
    doh[COLS:, :] = jnp.zeros((PAD, HEAD), BF16)
    for j in range(4, CTX):
        for t in range(CTX - j, 5):
            wts_t[j + 4, :, t * 128 : t * 128 + 128] = jnp.zeros((128, 128), BF16)
    dk_t[...] = jnp.zeros(dk_t.shape, F32)
    stamp_pad[:, 0:PAD] = jnp.zeros((1, PAD), jnp.int32)
    for copy in small_copies:
        copy.wait()
    stamp_pad[:, PAD:] = stamp_ref[...]

    reversed_pos = lanes_reversed(pos_ref[...])
    line = jnp.concatenate(
        [reversed_pos[4 - b : 5 - b, :] for b in range(5)] + [jnp.zeros((1, 128), F32)], axis=1
    )
    sheet = pltpu.roll(jnp.broadcast_to(line, (ROWS, 768)), 1, 1)
    row_no = lax.broadcasted_iota(jnp.int32, (ROWS, 768), 0)
    for bit in range(7):
        rolled = pltpu.roll(sheet, 1 << bit, 1)
        sheet = jnp.where((row_no & (1 << bit)) != 0, rolled, sheet)
    tz[...] = sheet[:, 128:]

    r_iota = lax.broadcasted_iota(jnp.int32, (ROWS, 128), 0)
    c_iota = lax.broadcasted_iota(jnp.int32, (ROWS, 128), 1)
    table = jnp.zeros((ROWS, 128), F32)
    for b in range(32):
        table = jnp.where(c_iota == b, time_ref[b], table)
    starts = []
    total = jnp.int32(0)
    for u in range(8):
        starts.append(total)
        total = total + len_ref[0, u]

    def bias_slab(i, unused):
        row_stamps = stamp_pad[:, pl.ds(aligned(PAD + i * ROWS), ROWS)]
        stamp_col = jnp.transpose(jnp.broadcast_to(row_stamps, (ROWS, 128)))
        place = r_iota + i * ROWS
        start = jnp.zeros((ROWS, 128), jnp.int32)
        for u in range(1, 8):
            start = jnp.where(place >= starts[u], jnp.maximum(start, starts[u]), start)
        first_col = start - (i * ROWS - PAD)
        numbers = []
        for b in range(5):
            key_stamps = stamp_pad[:, pl.ds(aligned(i * ROWS + b * 128), 128)]
            number = 32 - lax.clz(stamp_col - key_stamps)
            timed = jnp.take_along_axis(table, number, axis=1, mode="promise_in_bounds")
            col = c_iota + b * 128
            mask = (col >= first_col) & (col <= r_iota + PAD)
            cols = slice(b * 128, b * 128 + 128)
            bias[i, :, cols] = jnp.where(mask, tz[:, cols] + timed, MASKED)

            numbers.append(number)
            if b in (1, 2, 3):
                bucket[i, :, cols] = number
        bucket[i, :, 512:] = jnp.where(c_iota <= r_iota, numbers[4], numbers[0])
        return unused

    lax.fori_loop(0, CTX, bias_slab, 0)

    wy_copy().wait_recv()
    for k in range(1, NZ):
        wz_copy(1, k).start()
    own_copies[5].wait()
    for k in range(1, NZ):
        wz_copy(0, k).wait_recv()
    for k in range(1, NX):
        wx_copy(0, k).start()
    for k in range(1, NZ):
        wz_copy(1, k).wait_recv()
    for k in range(1, NX):
        wx_copy(1, k).start()
    wc_copy(0).start()

    for copy in own_copies[:5]:
        copy.wait()
    for a in (0, 1):
        for k in range(1, CTX):
            qkv_copy(a, k).wait_recv()

    def weigh(i, unused):
        rows = pl.ds(aligned(i * ROWS), ROWS)
        slab = pl.ds(aligned(i * ROWS), SLAB)
        pair_bias = bias[i]
        mask = pair_bias > 0.1 * MASKED
        scores = dot_nt(qh[rows, :], kh[slab, :]) * FACTOR + pair_bias
        sig = gate_of(scores)
        weights = jnp.where(mask, scores * sig, 0.0).astype(BF16)
        wts[i] = weights
        bias[i] = jnp.where(mask, sig * (1.0 + scores * (1.0 - sig)), 0.0)
        for b in range(5):
            turned = jnp.transpose(weights[:, b * 128 : b * 128 + 128])
            wts_t[i + b, :, (4 - b) * 128 : (5 - b) * 128] = turned
        q_t[:, rows] = jnp.transpose(qh[rows, :])
        return unused

    lax.fori_loop(0, CTX, weigh, 0)

    def attend(i):
        slab = pl.ds(aligned(i * ROWS), SLAB)
        return dot(wts[i], vh[slab, :]).astype(BF16)

    def part_rows(part):
        return pl.ds(part * 64, 64)

    def o_copy(part, k):
        where = ctx_peer(k)
        rows = part_rows(part)
        return remote(
            o_send.at[where[1], rows], o_row.at[rows, my_cols], o_s.at[part, k], o_r.at[part, k], where
        )

    def attend_step(k, unused):
        i = lax.rem(me + k, CTX)
        o_send[i] = attend(i)
        o_copy(0, k).start()
        return unused

    for k in range(1, CTX):
        qkv_copy(2, k).wait_recv()
    lax.fori_loop(1, CTX, attend_step, 0)
    for k in range(1, CTX):
        o_copy(1, k).start()
    o_row[:, my_cols] = attend(me)

    for k in range(1, NX):
        for which in range(2):
            wx_copy(which, k).wait_recv()
        wc_copy(k).start()
    for k in range(NX):
        wc_copy(k).wait_recv()

    def mixed_grad_part(n, unused):
        block = wbuf[n].reshape(256, COLS)
        mgrad[:, pl.ds(aligned(n * 256), 256)] = dot_nt(ograd[...], block)
        return unused

    lax.fori_loop(0, NX, mixed_grad_part, 0)

    def rows_part(n, unused):
        rows = pl.ds(aligned(n * 32, 32), 32)
        attended = o_row[rows, :].astype(F32)
        center = attended - jnp.mean(attended, axis=1, keepdims=True)
        inv_dev = lax.rsqrt(jnp.mean(center * center, axis=1, keepdims=True) + EPSILON)
        normed = center * inv_dev
        gate_wide = gate[rows, :].astype(F32)
        grad = mgrad[rows, :]
        mixed[rows, :] = (normed * gate_wide).astype(BF16)
        gg_v[rows, :] = (grad * normed).astype(BF16)
        normed_grad = grad * gate_wide
        first = jnp.mean(normed_grad, axis=1, keepdims=True)
        second = jnp.mean(normed_grad * normed, axis=1, keepdims=True)
        a_send[rows, :] = (inv_dev * (normed_grad - first - normed * second)).astype(BF16)
        return unused

    def a_copy(part, k):
        where = ctx_peer(k)
        cols = pl.ds(aligned(where[1] * HEAD), HEAD)
        rows = pl.ds(aligned(me * ROWS + part * 64, 64), 64)
        return remote(
            a_send.at[part_rows(part), cols], doh.at[rows], a_s.at[part, k], a_r.at[part, k], where
        )

    for part in range(2):
        for k in range(1, CTX):
            o_copy(part, k).wait_recv()
        lax.fori_loop(2 * part, 2 * part + 2, rows_part, 0)
        for k in range(1, CTX):
            a_copy(part, k).start()
    doh[my_rows, :] = a_send[:, my_cols]

    other_half = pl.ds(aligned((1 - core) * 512), 512)

    def rc_copy(k):
        part = lax.rem(x + k, NX)
        return remote(w_send.at[part], w_r0.at[part], rc_s.at[k], rc_r.at[k], (dp, yh * 2 + 1 - core))

    def weight_part(k, unused):
        part = lax.rem(x + k, NX)
        turned = jnp.transpose(mixed[:, pl.ds(aligned(part * 256), 256)])
        w_send[part] = dot(turned, ograd[:, other_half]).astype(BF16).reshape(2, 128, 512)
        rc_copy(k).start()
        w_own[part] = dot(turned, ograd[:, half]).reshape(2, 128, 512)
        return unused

    lax.fori_loop(1, NX + 1, weight_part, 0)

    wide, narrow_cols = pl.ds(0, 384), pl.ds(384, 128)

    def z_rows(k):
        return pl.ds(aligned(lax.rem(z + k, NZ) * WROWS, WROWS), WROWS)

    def ax_copy(k):
        part = lax.rem(x + k, NX)
        return remote(w_s0.at[part, :, :, wide], w_ax.at[k], rx_s.at[0, k], rx_r.at[0, k], x_peer(k))

    def az_copy(k):
        return remote(w_a1.at[:, z_rows(k)], w_az.at[k], rz_s.at[0, k], rz_r.at[0, k], z_peer(k))

    def bz_copy(k):
        src = w_s0.at[:, :, z_rows(k), narrow_cols]
        return remote(src, w_bz.at[k], rz_s.at[1, k], rz_r.at[1, k], z_peer(k))

    def bx_copy(k):
        part = lax.rem(x + k, NX)
        return remote(w_b1.at[part], w_bx.at[k], rx_s.at[1, k], rx_r.at[1, k], x_peer(k))

    def core_sum(k):
        part = lax.rem(x + k, NX)
        rc_copy(k).wait_recv()
        w_s0[part] = (w_own[part] + w_r0[part].astype(F32)).astype(BF16)

    def core_step(k, unused):
        core_sum(k)
        ax_copy(k).start()
        return unused

    lax.fori_loop(1, NX, core_step, 0)
    core_sum(NX)
    for k in range(1, NZ):
        bz_copy(k).start()

    def layer_part(n, unused):
        cols = pl.ds(aligned(n * 256), 256)
        block = wbuf[:, :, :, cols].reshape(COLS, 256)
        lo_v[:, cols] = dot(mixed[...], block).astype(BF16)
        return unused

    lax.fori_loop(0, 4, layer_part, 0)
    out_copies = [
        pltpu.make_async_copy(lo_v, lo_out.at[0], loc.at[6]),
        pltpu.make_async_copy(gg_v, gg_out.at[0], loc.at[7]),
    ]
    for copy in out_copies:
        copy.start()


    for part in range(2):
        for k in range(1, CTX):
            a_copy(part, k).wait_recv()

    outs = (dq_out, dk_out, dv_out)

    def d_copy(a, k):
        where = ctx_peer(k)
        return remote(d_send.at[a, where[1]], outs[a].at[0, :, my_cols], d_s.at[a, k], d_r.at[a, k], where)

    def value_block(i):
        slab = pl.ds(aligned(i * ROWS), SLAB)
        d_send[2, i] = dot(wts_t[i + 4], doh[slab, :]).astype(BF16)

    def value_step(k, unused):
        value_block(lax.rem(me + k, CTX))
        d_copy(2, k).start()
        return unused

    lax.fori_loop(1, CTX, value_step, 0)
    value_block(me)

    def query_block(i):
        rows = pl.ds(aligned(i * ROWS), ROWS)
        slab = pl.ds(aligned(i * ROWS), SLAB)
        score_grad = dot_nt(doh[rows, :], vh[slab, :]) * bias[i]
        bias[i] = score_grad
        narrow = score_grad.astype(BF16)
        dk_t[:, slab] += dot(q_t[:, rows], narrow)
        d_send[0, i] = (dot(narrow, kh[slab, :]) * FACTOR).astype(BF16)

    def query_step(k, unused):
        query_block(lax.rem(me + k, CTX))
        d_copy(0, k).start()
        return unused

    lax.fori_loop(1, CTX, query_step, 0)
    query_block(me)

    pos_fold[:, 0:128] = jnp.zeros((ROWS, 128), F32)

    def slab_sum(n, unused):
        rows = pl.ds(aligned(n * 8, 8), 8)
        total = bias[0, rows, :]
        for i in range(1, CTX):
            total = total + bias[i, rows, :]
        pos_fold[rows, 128:] = total
        return unused

    lax.fori_loop(0, 16, slab_sum, 0)
    fold = pos_fold[...]
    for count in (64, 32, 16, 8):
        fold = fold[:count] + pltpu.roll(fold[count : 2 * count], 768 - count, 1)
    row_no = lax.broadcasted_iota(jnp.int32, (8, 768), 0)
    for count in (4, 2, 1):
        fold = jnp.where((row_no & count) != 0, pltpu.roll(fold, 768 - count, 1), fold)
    fold = pltpu.roll(fold, 767, 1)
    fold = jnp.broadcast_to(jnp.sum(fold, axis=0, keepdims=True), (8, 768))
    row8 = lax.broadcasted_iota(jnp.int32, (8, 128), 0)
    sums = jnp.zeros((8, 128), F32)
    for b in range(4):
        block = lanes_reversed(fold[:, (4 - b) * 128 : (5 - b) * 128])
        sums = jnp.where(row8 == b, block, sums)

    def histogram(first, blocks):
        def step(n, totals):
            i = first + lax.div(n, 16)
            rows = pl.ds(aligned(lax.rem(n, 16) * 8, 8), 8)
            grads = [bias[i, rows, 0:128] + bias[i, rows, 512:640]]
            numbers = [bucket[i, rows, 512:640]]
            for b in blocks:
                grads.append(bias[i, rows, b * 128 : b * 128 + 128])
                numbers.append(bucket[i, rows, b * 128 : b * 128 + 128])
            out = []
            for number in range(BUCKETS):
                part = totals[number]
                for at in range(len(grads)):
                    part = part + jnp.where(numbers[at] == number, grads[at], 0.0)
                out.append(part)
            return tuple(out)

        return step

    totals = tuple(jnp.zeros((8, 128), F32) for unused in range(BUCKETS))
    for first, count, blocks in ((0, 1, ()), (1, 1, (3,)), (2, 1, (2, 3)), (3, 1, (1, 2, 3))):
        totals = lax.fori_loop(0, 16 * count, histogram(first, blocks), totals)
    for k in range(1, NX):
        ax_copy(k).wait_recv()

    def a_sum(n, unused):
        to_yl = lax.div(n, 4)
        rows = pl.ds(aligned(lax.rem(n, 4) * 32, 32), 32)
        total = w_own[x, to_yl, rows, wide] + w_r0[x, to_yl, rows, wide].astype(F32)
        for k in range(1, NX):
            total = total + w_ax[k, to_yl, rows, :].astype(F32)
        w_a1[to_yl, rows, :] = total.astype(BF16)
        return unused

    lax.fori_loop(0, 8, a_sum, 0)
    for k in range(1, NZ):
        az_copy(k).start()
    for k in range(1, NZ):
        bz_copy(k).wait_recv()

    def b_sum(n, unused):
        total = w_own[n, :, z_rows(0), narrow_cols] + w_r0[n, :, z_rows(0), narrow_cols].astype(F32)
        for k in range(1, NZ):
            total = total + w_bz[k, n].astype(F32)
        w_b1[n] = total.astype(BF16)
        return unused

    lax.fori_loop(0, NX, b_sum, 0)
    for k in range(1, NX):
        bx_copy(k).start()

    totals = lax.fori_loop(0, 16 * 4, histogram(4, (1, 2, 3)), totals)
    lane8 = lax.broadcasted_iota(jnp.int32, (8, 128), 1)
    timed = jnp.zeros((8, 128), F32)
    for b in range(BUCKETS):
        whole = jnp.sum(jnp.sum(totals[b], axis=0, keepdims=True), axis=1, keepdims=True)
        timed = jnp.where(lane8 == b, whole, timed)
    sums = jnp.where(row8 == 4, timed, sums)

    slots = (me, z, x * NYL + yl)
    b_peers = (ctx_peer, z_peer, xy_peer)

    def b_copy(level, k):
        return remote(b_v.at[level], b_r.at[level, slots[level]], b_s.at[level, k], b_rs.at[level, k], b_peers[level](k))

    def b_start(level, value):
        b_v[level] = value
        b_r[level, slots[level]] = value
        for k in range(1, 8):
            b_copy(level, k).start()

    def b_finish(level):
        for k in range(1, 8):
            b_copy(level, k).wait_recv()
        value = b_r[level, 0]
        for slot in range(1, 8):
            value = value + b_r[level, slot]
        return value

    b_start(0, sums)

    def key_block(i):
        rows = pl.ds(aligned(PAD + i * ROWS), ROWS)
        d_send[1, i] = (jnp.transpose(dk_t[:, rows]) * FACTOR).astype(BF16)

    def key_step(k, unused):
        key_block(lax.rem(me + k, CTX))
        d_copy(1, k).start()
        return unused

    lax.fori_loop(1, CTX, key_step, 0)
    key_block(me)
    d_own = [
        pltpu.make_async_copy(d_send.at[a, me], outs[a].at[0, :, my_cols], loc.at[8 + a])
        for a in range(3)
    ]
    for copy in d_own:
        copy.start()

    def ry_copy(k):
        to_yl = lax.rem(yl + k // NYH, NYL)
        cols = pl.ds(aligned(lax.rem(yh + k % NYH, NYH) * 128), 128)
        return remote(w_s2.at[to_yl, :, cols], w_r3.at[k], ry_s.at[k], ry_r.at[k], y_peer(k))

    for k in range(1, NZ):
        az_copy(k).wait_recv()
    total = w_a1[:, z_rows(0), :].astype(F32)
    for k in range(1, NZ):
        total = total + w_az[k].astype(F32)
    w_s2[:, :, wide] = total
    for k in range(1, NX):
        bx_copy(k).wait_recv()
    total = w_b1[x].astype(F32)
    for k in range(1, NX):
        total = total + w_bx[k].astype(F32)
    w_s2[:, :, narrow_cols] = total
    for k in range(1, NYL * NYH):
        ry_copy(k).start()

    b_start(1, b_finish(0))

    for k in range(1, NYL * NYH):
        ry_copy(k).wait_recv()
    piece = w_s2[yl, :, pl.ds(aligned(yh * 128), 128)]
    for k in range(1, NYL * NYH):
        piece = piece + w_r3[k]
    w_s3[...] = piece
    piece_cols = pl.ds(aligned(core * 512 + yh * 128), 128)
    w_land[:, piece_cols] = piece

    def ag_copy(k):
        return remote(w_s3, w_land.at[:, piece_cols], ag_s.at[k], ag_r.at[k], ctx_peer(k))

    for k in range(1, CTX):
        ag_copy(k).start()

    b_start(2, b_finish(1))

    for k in range(1, CTX):
        ag_copy(k).wait_recv()
    wg_copy = pltpu.make_async_copy(w_land, wg_out, loc.at[15])
    wg_copy.start()

    sums = b_finish(2)
    table_v[0] = jnp.where(row8 < 4, sums, 0.0)
    table_v[1] = jnp.broadcast_to(sums[4:5, :], (8, 128))
    table_copies = [
        pltpu.make_async_copy(table_v.at[0], pos_out, loc.at[16]),
        pltpu.make_async_copy(table_v.at[1], time_out, loc.at[17]),
    ]
    for copy in table_copies:
        copy.start()

    for k in range(1, CTX):
        for a in range(3):
            qkv_copy(a, k).wait_send()
            b_copy(a, k).wait_send()
        for part in range(2):
            wz_copy(part, k).wait_send()
            o_copy(part, k).wait_send()
            a_copy(part, k).wait_send()
        az_copy(k).wait_send()
        bz_copy(k).wait_send()
        ry_copy(k).wait_send()
        ag_copy(k).wait_send()
    for k in range(1, NX):
        for which in range(2):
            wx_copy(which, k).wait_send()
        ax_copy(k).wait_send()
        bx_copy(k).wait_send()
    for k in range(1, NX + 1):
        rc_copy(k).wait_send()
    for k in range(NX):
        wc_copy(k).wait_send()
    wy_copy().wait_send()
    for copy in d_own + out_copies + table_copies + [wg_copy]:
        copy.wait()
    for a in (2, 0, 1):
        for k in range(1, CTX):
            d_copy(a, k).wait_recv()
            d_copy(a, k).wait_send()


def hand_over(*refs):
    given, results, held, sems = refs[:7], refs[8:15], refs[16:23], refs[23]
    reads = [pltpu.make_async_copy(given[n], held[n], sems.at[0, n]) for n in range(7)]
    writes = [pltpu.make_async_copy(held[n], results[n], sems.at[1, n]) for n in range(7)]
    for copy in reads:
        copy.start()
    refs[15][...] = refs[7][0, 0:32]
    for read, write in zip(reads, writes):
        read.wait()
        write.start()
    for copy in writes:
        copy.wait()


def on_device(
    query_in, key_in, value_in, gate_in, out_grad, out_weight, lengths, stamps, pos_bias, time_bias
):
    dma = lambda *shape: pltpu.SemaphoreType.DMA(shape)
    vmem = pltpu.VMEM
    anywhere = pl.BlockSpec(memory_space=pl.ANY)
    in_vmem = pl.BlockSpec(memory_space=pltpu.VMEM)
    rows_shape = jax.ShapeDtypeStruct((1, ROWS, COLS), BF16)
    outs = pl.pallas_call(
        kernel,
        out_shape=[rows_shape] * 5
        + [
            jax.ShapeDtypeStruct((WROWS, COLS), F32),
            jax.ShapeDtypeStruct((8, 128), F32),
            jax.ShapeDtypeStruct((8, 128), F32),
        ],
        in_specs=[anywhere] * 10,
        out_specs=[anywhere] * 8,
        scratch_shapes=[
            pltpu.SMEM((1, 8), jnp.int32),
            vmem((1, COLS), jnp.int32),
            vmem((8, 128), F32),
            pltpu.SMEM((32,), F32),
            vmem((2, 8, 128), F32),
            vmem((COLS, HEAD), BF16),
            vmem((PAD + COLS, HEAD), BF16),
            vmem((PAD + COLS, HEAD), BF16),
            vmem((COLS + PAD, HEAD), BF16),
            vmem((CTX, ROWS, HEAD), BF16),
            vmem((ROWS, COLS), BF16),
            vmem((ROWS, COLS), BF16),
            vmem((ROWS, COLS), BF16),
            vmem((ROWS, COLS), BF16),
            vmem((ROWS, COLS), BF16),
            vmem((ROWS, COLS), F32),
            vmem((NX, NYL, NZ * WROWS, COLS), BF16),
            vmem((1, PAD + COLS), jnp.int32),
            vmem((ROWS, SLAB), F32),
            vmem((CTX, ROWS, SLAB), F32),
            vmem((CTX, ROWS, SLAB), jnp.int32),
            vmem((CTX, ROWS, SLAB), BF16),
            vmem((CTX + 4, ROWS, SLAB), BF16),
            vmem((HEAD, COLS), BF16),
            vmem((HEAD, PAD + COLS), F32),
            vmem((3, CTX, ROWS, HEAD), BF16),
            vmem((ROWS, 768), F32),
            vmem((ROWS, COLS), BF16),
            vmem((ROWS, COLS), BF16),
            vmem((NX, NYL, 128, 512), BF16),
            vmem((NX, NYL, 128, 512), F32),
            vmem((NX, NYL, 128, 512), BF16),
            vmem((NX, NYL, 128, 512), BF16),
            vmem((NX, NYL, 128, 384), BF16),
            vmem((NYL, 128, 384), BF16),
            vmem((NZ, NYL, WROWS, 384), BF16),
            vmem((NZ, NX, NYL, WROWS, 128), BF16),
            vmem((NX, NYL, WROWS, 128), BF16),
            vmem((NX, NYL, WROWS, 128), BF16),
            vmem((NYL, WROWS, 512), F32),
            vmem((NYL * NYH, WROWS, 128), F32),
            vmem((WROWS, 128), F32),
            vmem((WROWS, COLS), F32),
            vmem((3, 8, 128), F32),
            vmem((3, 8, 8, 128), F32),
            dma(18),
            dma(3, 8), dma(3, 8),
            dma(2, 8), dma(2, 8),
            dma(2, 4), dma(2, 4),
            dma(1), dma(1),
            dma(4), dma(4),
            dma(2, 8), dma(2, 8),
            dma(2, 8), dma(2, 8),
            dma(3, 8), dma(3, 8),
            dma(5), dma(5),
            dma(2, 4), dma(2, 4),
            dma(2, 8), dma(2, 8),
            dma(8), dma(8),
            dma(8), dma(8),
            dma(3, 8), dma(3, 8),
        ],
        compiler_params=pltpu.CompilerParams(
            collective_id=0, has_side_effects=True, vmem_limit_bytes=56 * 1024 * 1024
        ),
    )(
        query_in,
        key_in,
        value_in,
        gate_in,
        out_grad,
        out_weight,
        lengths,
        stamps,
        pos_bias.reshape(8, 128),
        time_bias,
    )
    outs = pl.pallas_call(
        hand_over,
        out_shape=[jax.ShapeDtypeStruct(out.shape, out.dtype) for out in outs[:7]]
        + [jax.ShapeDtypeStruct((32,), F32)],
        in_specs=[anywhere] * 7 + [in_vmem],
        out_specs=[anywhere] * 7 + [in_vmem],
        scratch_shapes=[vmem(out.shape, out.dtype) for out in outs[:7]] + [dma(2, 7)],
        compiler_params=pltpu.CompilerParams(vmem_limit_bytes=56 * 1024 * 1024),
    )(*outs)
    layer_out, query_grad, key_grad, value_grad, gate_grad, weight_grad, pos, timed = outs
    return (
        layer_out,
        query_grad,
        key_grad,
        value_grad,
        gate_grad,
        weight_grad,
        pos.reshape(COLS),
        timed,
    )


def solution(mesh):
    rows = P("dp", "ctx", None)
    owned = P("dp", None)
    return jax.shard_map(
        on_device,
        mesh=mesh,
        in_specs=(rows, rows, rows, rows, rows, owned, owned, owned, P(), P()),
        out_specs=(rows, rows, rows, rows, rows, owned, P(), P()),
        check_vma=False,
    )
```

```python
import functools

import jax
import jax.numpy as jnp
from jax import lax
from jax.experimental import pallas as pl
from jax.experimental.pallas import tpu as pltpu
from jax.sharding import PartitionSpec as P

HEAD = 128
ROWS = 128
CTX = 8
COLS = 1024
PAD = 512
SLAB = PAD + ROWS
NX, NYL, NZ, NYH = 4, 2, 8, 4
WROWS = 16
EPSILON = 1e-06
FACTOR = HEAD ** (-0.5)
MASKED = -1e30
BUCKETS = 24
F32 = jnp.float32
BF16 = jnp.bfloat16
NT = (((1,), (1,)), ((), ()))


def dot(a, b):
    return jnp.dot(a, b, preferred_element_type=F32)


def dot_nt(a, b):
    return lax.dot_general(a, b, NT, preferred_element_type=F32)


def aligned(start, size=128):
    return pl.multiple_of(start, size)


def lanes_reversed(block):
    lane = lax.broadcasted_iota(jnp.int32, block.shape, 1)
    return jnp.take_along_axis(block, 127 - lane, axis=1, mode="promise_in_bounds")


def gate_of(scores):
    return 0.5 * jnp.tanh(0.5 * scores) + 0.5


def kernel(
    q_in, k_in, v_in, g_in, og_in, w_in, len_in, stamp_in, pos_in, time_in,
    lo_out, dq_out, dk_out, dv_out, gg_out, wg_out, pos_out, time_out,
    len_ref, stamp_ref, pos_ref, time_ref, table_v,
    qh, kh, vh, doh, o_send, o_row, a_send, gate, ograd, mixed, mgrad, wbuf,
    stamp_pad, tz, bias, bucket, wts, wts_t, q_t, dk_t, d_send, pos_fold,
    lo_v, gg_v, w_send, w_own, w_r0, w_s0, w_ax, w_a1, w_az, w_bz, w_b1, w_bx, w_s2, w_r3, w_land,
    b_v, b_r,
    loc, qkv_s, qkv_r, wz_s, wz_r, wx_s, wx_r, wy_s, wy_r, wc_s, wc_r,
    o_s, o_r, a_s, a_r, d_s, d_r, rc_s, rc_r, rx_s, rx_r, rz_s, rz_r, ry_s, ry_r,
    ag_s, ag_r, b_s, b_rs,
):
    dp = lax.axis_index("dp")
    me = lax.axis_index("ctx")
    z = lax.rem(dp, NZ)
    yl = lax.rem(lax.div(dp, NZ), NYL)
    x = lax.div(dp, NZ * NYL)
    core = lax.rem(me, 2)
    yh = lax.div(me, 2)

    def dp_of(xx, yy, zz):
        return (xx * NYL + yy) * NZ + zz

    def ctx_peer(k):
        return (dp, lax.rem(me + k, CTX))

    def z_peer(k):
        return (dp_of(x, yl, lax.rem(z + k, NZ)), me)

    def x_peer(k):
        return (dp_of(lax.rem(x + k, NX), yl, z), me)

    def xy_peer(k):
        return (dp_of(lax.rem(x + k // 2, NX), lax.rem(yl + k % 2, NYL), z), me)

    def y_peer(k):
        return (dp_of(x, lax.rem(yl + k // NYH, NYL), z), lax.rem(yh + k % NYH, NYH) * 2 + core)

    def remote(src, dst, send_sem, recv_sem, where):
        return pltpu.make_async_remote_copy(
            src_ref=src,
            dst_ref=dst,
            send_sem=send_sem,
            recv_sem=recv_sem,
            device_id=where,
            device_id_type=pl.DeviceIdType.MESH,
        )

    partners = [ctx_peer(k) for k in range(1, CTX)]
    partners += [z_peer(k) for k in range(1, NZ)]
    partners += [xy_peer(k) for k in range(1, NX * NYL)]
    partners += [y_peer(NYH + k) for k in range(1, NYH)]
    barrier = pltpu.get_barrier_semaphore()
    for where in partners:
        pl.semaphore_signal(barrier, inc=1, device_id=where, device_id_type=pl.DeviceIdType.MESH)

    my_rows = pl.ds(aligned(me * ROWS), ROWS)
    my_pad_rows = pl.ds(aligned(PAD + me * ROWS), ROWS)
    my_cols = pl.ds(aligned(me * HEAD), HEAD)
    half = pl.ds(aligned(core * 512), 512)
    w_rows = pl.ds(aligned(z * WROWS, WROWS), WROWS)
    own_copies = [
        pltpu.make_async_copy(q_in.at[0, :, my_cols], qh.at[my_rows], loc.at[0]),
        pltpu.make_async_copy(k_in.at[0, :, my_cols], kh.at[my_pad_rows], loc.at[1]),
        pltpu.make_async_copy(v_in.at[0, :, my_cols], vh.at[my_pad_rows], loc.at[2]),
        pltpu.make_async_copy(g_in.at[0], gate, loc.at[3]),
        pltpu.make_async_copy(og_in.at[0], ograd, loc.at[4]),
        pltpu.make_async_copy(w_in.at[:, half], wbuf.at[x, yl, w_rows, half], loc.at[5]),
    ]
    small_copies = [
        pltpu.make_async_copy(len_in, len_ref, loc.at[11]),
        pltpu.make_async_copy(stamp_in, stamp_ref, loc.at[12]),
        pltpu.make_async_copy(pos_in, pos_ref, loc.at[13]),
        pltpu.make_async_copy(time_in, time_ref, loc.at[14]),
    ]
    for copy in small_copies:
        copy.start()
    pl.semaphore_wait(barrier, len(partners))

    def qkv_copy(a, k):
        where = ctx_peer(k)
        cols = pl.ds(aligned(where[1] * HEAD), HEAD)
        src = (q_in, k_in, v_in)[a].at[0, :, cols]
        dst = (qh.at[my_rows], kh.at[my_pad_rows], vh.at[my_pad_rows])[a]
        return remote(src, dst, qkv_s.at[a, k], qkv_r.at[a, k], where)

    def wy_copy():
        return remote(w_in.at[:, half], wbuf.at[x, yl, w_rows, half], wy_s.at[0], wy_r.at[0], (dp_of(x, 1 - yl, z), me))

    def wz_copy(which, k):
        dst = wbuf.at[x, yl if which == 0 else 1 - yl, w_rows, half]
        src = w_in.at[:, half] if which == 0 else dst
        return remote(src, dst, wz_s.at[which, k], wz_r.at[which, k], z_peer(k))

    def wx_copy(which, k):
        part = wbuf.at[x, yl if which == 0 else 1 - yl, :, half]
        return remote(part, part, wx_s.at[which, k], wx_r.at[which, k], x_peer(k))

    def wc_copy(k):
        part = wbuf.at[lax.rem(x + NX - k, NX), :, :, half]
        return remote(part, part, wc_s.at[k], wc_r.at[k], (dp, yh * 2 + 1 - core))

    wy_copy().start()
    for k in range(1, NZ):
        wz_copy(0, k).start()
    for k in (3, 4, 5, 2, 6, 1, 7):
        qkv_copy(0, k).start()
        qkv_copy(1, k).start()
    for copy in own_copies:
        copy.start()
    for k in (3, 4, 5, 2, 6, 1, 7):
        qkv_copy(2, k).start()
    kh[0:PAD, :] = jnp.zeros((PAD, HEAD), BF16)
    vh[0:PAD, :] = jnp.zeros((PAD, HEAD), BF16)
    doh[COLS:, :] = jnp.zeros((PAD, HEAD), BF16)
    for j in range(4, CTX):
        for t in range(CTX - j, 5):
            wts_t[j + 4, :, t * 128 : t * 128 + 128] = jnp.zeros((128, 128), BF16)
    dk_t[...] = jnp.zeros(dk_t.shape, F32)
    stamp_pad[:, 0:PAD] = jnp.zeros((1, PAD), jnp.int32)
    for copy in small_copies:
        copy.wait()
    stamp_pad[:, PAD:] = stamp_ref[...]

    reversed_pos = lanes_reversed(pos_ref[...])
    line = jnp.concatenate(
        [reversed_pos[4 - b : 5 - b, :] for b in range(5)] + [jnp.zeros((1, 128), F32)], axis=1
    )
    sheet = pltpu.roll(jnp.broadcast_to(line, (ROWS, 768)), 1, 1)
    row_no = lax.broadcasted_iota(jnp.int32, (ROWS, 768), 0)
    for bit in range(7):
        rolled = pltpu.roll(sheet, 1 << bit, 1)
        sheet = jnp.where((row_no & (1 << bit)) != 0, rolled, sheet)
    tz[...] = sheet[:, 128:]

    r_iota = lax.broadcasted_iota(jnp.int32, (ROWS, 128), 0)
    c_iota = lax.broadcasted_iota(jnp.int32, (ROWS, 128), 1)
    table = jnp.zeros((ROWS, 128), F32)
    for b in range(32):
        table = jnp.where(c_iota == b, time_ref[b], table)
    starts = []
    total = jnp.int32(0)
    for u in range(8):
        starts.append(total)
        total = total + len_ref[0, u]

    def bias_slab(i, unused):
        row_stamps = stamp_pad[:, pl.ds(aligned(PAD + i * ROWS), ROWS)]
        stamp_col = jnp.transpose(jnp.broadcast_to(row_stamps, (ROWS, 128)))
        place = r_iota + i * ROWS
        start = jnp.zeros((ROWS, 128), jnp.int32)
        for u in range(1, 8):
            start = jnp.where(place >= starts[u], jnp.maximum(start, starts[u]), start)
        first_col = start - (i * ROWS - PAD)
        numbers = []
        for b in range(5):
            key_stamps = stamp_pad[:, pl.ds(aligned(i * ROWS + b * 128), 128)]
            number = 32 - lax.clz(stamp_col - key_stamps)
            timed = jnp.take_along_axis(table, number, axis=1, mode="promise_in_bounds")
            col = c_iota + b * 128
            mask = (col >= first_col) & (col <= r_iota + PAD)
            cols = slice(b * 128, b * 128 + 128)
            bias[i, :, cols] = jnp.where(mask, tz[:, cols] + timed, MASKED)

            numbers.append(number)
            if b in (1, 2, 3):
                bucket[i, :, cols] = number
        bucket[i, :, 512:] = jnp.where(c_iota <= r_iota, numbers[4], numbers[0])
        return unused

    lax.fori_loop(0, CTX, bias_slab, 0)

    wy_copy().wait_recv()
    for k in range(1, NZ):
        wz_copy(1, k).start()
    own_copies[5].wait()
    for k in range(1, NZ):
        wz_copy(0, k).wait_recv()
    for k in range(1, NX):
        wx_copy(0, k).start()
    for k in range(1, NZ):
        wz_copy(1, k).wait_recv()
    for k in range(1, NX):
        wx_copy(1, k).start()
    wc_copy(0).start()

    for copy in own_copies[:5]:
        copy.wait()
    for a in (0, 1):
        for k in range(1, CTX):
            qkv_copy(a, k).wait_recv()

    def weigh(i, unused):
        rows = pl.ds(aligned(i * ROWS), ROWS)
        slab = pl.ds(aligned(i * ROWS), SLAB)
        pair_bias = bias[i]
        mask = pair_bias > 0.1 * MASKED
        scores = dot_nt(qh[rows, :], kh[slab, :]) * FACTOR + pair_bias
        sig = gate_of(scores)
        weights = jnp.where(mask, scores * sig, 0.0).astype(BF16)
        wts[i] = weights
        bias[i] = jnp.where(mask, sig * (1.0 + scores * (1.0 - sig)), 0.0)
        for b in range(5):
            turned = jnp.transpose(weights[:, b * 128 : b * 128 + 128])
            wts_t[i + b, :, (4 - b) * 128 : (5 - b) * 128] = turned
        q_t[:, rows] = jnp.transpose(qh[rows, :])
        return unused

    lax.fori_loop(0, CTX, weigh, 0)

    def attend(i):
        slab = pl.ds(aligned(i * ROWS), SLAB)
        return dot(wts[i], vh[slab, :]).astype(BF16)

    def part_rows(part):
        return pl.ds(part * 64, 64)

    def o_copy(part, k):
        where = ctx_peer(k)
        rows = part_rows(part)
        return remote(
            o_send.at[where[1], rows], o_row.at[rows, my_cols], o_s.at[part, k], o_r.at[part, k], where
        )

    def attend_step(k, unused):
        i = lax.rem(me + k, CTX)
        o_send[i] = attend(i)
        o_copy(0, k).start()
        return unused

    for k in range(1, CTX):
        qkv_copy(2, k).wait_recv()
    lax.fori_loop(1, CTX, attend_step, 0)
    for k in range(1, CTX):
        o_copy(1, k).start()
    o_row[:, my_cols] = attend(me)

    for k in range(1, NX):
        for which in range(2):
            wx_copy(which, k).wait_recv()
        wc_copy(k).start()
    for k in range(NX):
        wc_copy(k).wait_recv()

    def mixed_grad_part(n, unused):
        block = wbuf[n].reshape(256, COLS)
        mgrad[:, pl.ds(aligned(n * 256), 256)] = dot_nt(ograd[...], block)
        return unused

    lax.fori_loop(0, NX, mixed_grad_part, 0)

    def rows_part(n, unused):
        rows = pl.ds(aligned(n * 32, 32), 32)
        attended = o_row[rows, :].astype(F32)
        center = attended - jnp.mean(attended, axis=1, keepdims=True)
        inv_dev = lax.rsqrt(jnp.mean(center * center, axis=1, keepdims=True) + EPSILON)
        normed = center * inv_dev
        gate_wide = gate[rows, :].astype(F32)
        grad = mgrad[rows, :]
        mixed[rows, :] = (normed * gate_wide).astype(BF16)
        gg_v[rows, :] = (grad * normed).astype(BF16)
        normed_grad = grad * gate_wide
        first = jnp.mean(normed_grad, axis=1, keepdims=True)
        second = jnp.mean(normed_grad * normed, axis=1, keepdims=True)
        a_send[rows, :] = (inv_dev * (normed_grad - first - normed * second)).astype(BF16)
        return unused

    def a_copy(part, k):
        where = ctx_peer(k)
        cols = pl.ds(aligned(where[1] * HEAD), HEAD)
        rows = pl.ds(aligned(me * ROWS + part * 64, 64), 64)
        return remote(
            a_send.at[part_rows(part), cols], doh.at[rows], a_s.at[part, k], a_r.at[part, k], where
        )

    for part in range(2):
        for k in range(1, CTX):
            o_copy(part, k).wait_recv()
        lax.fori_loop(2 * part, 2 * part + 2, rows_part, 0)
        for k in range(1, CTX):
            a_copy(part, k).start()
    doh[my_rows, :] = a_send[:, my_cols]

    other_half = pl.ds(aligned((1 - core) * 512), 512)

    def rc_copy(k):
        part = lax.rem(x + k, NX)
        return remote(w_send.at[part], w_r0.at[part], rc_s.at[k], rc_r.at[k], (dp, yh * 2 + 1 - core))

    def weight_part(k, unused):
        part = lax.rem(x + k, NX)
        turned = jnp.transpose(mixed[:, pl.ds(aligned(part * 256), 256)])
        w_send[part] = dot(turned, ograd[:, other_half]).astype(BF16).reshape(2, 128, 512)
        rc_copy(k).start()
        w_own[part] = dot(turned, ograd[:, half]).reshape(2, 128, 512)
        return unused

    lax.fori_loop(1, NX + 1, weight_part, 0)

    wide, narrow_cols = pl.ds(0, 384), pl.ds(384, 128)

    def z_rows(k):
        return pl.ds(aligned(lax.rem(z + k, NZ) * WROWS, WROWS), WROWS)

    def ax_copy(k):
        part = lax.rem(x + k, NX)
        return remote(w_s0.at[part, :, :, wide], w_ax.at[k], rx_s.at[0, k], rx_r.at[0, k], x_peer(k))

    def az_copy(k):
        return remote(w_a1.at[:, z_rows(k)], w_az.at[k], rz_s.at[0, k], rz_r.at[0, k], z_peer(k))

    def bz_copy(k):
        src = w_s0.at[:, :, z_rows(k), narrow_cols]
        return remote(src, w_bz.at[k], rz_s.at[1, k], rz_r.at[1, k], z_peer(k))

    def bx_copy(k):
        part = lax.rem(x + k, NX)
        return remote(w_b1.at[part], w_bx.at[k], rx_s.at[1, k], rx_r.at[1, k], x_peer(k))

    def core_sum(k):
        part = lax.rem(x + k, NX)
        rc_copy(k).wait_recv()
        w_s0[part] = (w_own[part] + w_r0[part].astype(F32)).astype(BF16)

    def core_step(k, unused):
        core_sum(k)
        ax_copy(k).start()
        return unused

    lax.fori_loop(1, NX, core_step, 0)
    core_sum(NX)
    for k in range(1, NZ):
        bz_copy(k).start()

    def layer_part(n, unused):
        cols = pl.ds(aligned(n * 256), 256)
        block = wbuf[:, :, :, cols].reshape(COLS, 256)
        lo_v[:, cols] = dot(mixed[...], block).astype(BF16)
        return unused

    lax.fori_loop(0, 4, layer_part, 0)
    out_copies = [
        pltpu.make_async_copy(lo_v, lo_out.at[0], loc.at[6]),
        pltpu.make_async_copy(gg_v, gg_out.at[0], loc.at[7]),
    ]
    for copy in out_copies:
        copy.start()


    for part in range(2):
        for k in range(1, CTX):
            a_copy(part, k).wait_recv()

    outs = (dq_out, dk_out, dv_out)

    def d_copy(a, k):
        where = ctx_peer(k)
        return remote(d_send.at[a, where[1]], outs[a].at[0, :, my_cols], d_s.at[a, k], d_r.at[a, k], where)

    def query_block(i):
        rows = pl.ds(aligned(i * ROWS), ROWS)
        slab = pl.ds(aligned(i * ROWS), SLAB)
        score_grad = dot_nt(doh[rows, :], vh[slab, :]) * bias[i]
        bias[i] = score_grad
        narrow = score_grad.astype(BF16)
        dk_t[:, slab] += dot(q_t[:, rows], narrow)
        d_send[0, i] = (dot(narrow, kh[slab, :]) * FACTOR).astype(BF16)

    def query_step(k, unused):
        query_block(lax.rem(me + k, CTX))
        d_copy(0, k).start()
        return unused

    lax.fori_loop(1, CTX, query_step, 0)
    query_block(me)

    def key_block(i):
        rows = pl.ds(aligned(PAD + i * ROWS), ROWS)
        d_send[1, i] = (jnp.transpose(dk_t[:, rows]) * FACTOR).astype(BF16)

    def key_step(k, unused):
        key_block(lax.rem(me + k, CTX))
        d_copy(1, k).start()
        return unused

    lax.fori_loop(1, CTX, key_step, 0)
    key_block(me)
    pos_fold[:, 0:128] = jnp.zeros((ROWS, 128), F32)

    def slab_sum(n, unused):
        rows = pl.ds(aligned(n * 8, 8), 8)
        total = bias[0, rows, :]
        for i in range(1, CTX):
            total = total + bias[i, rows, :]
        pos_fold[rows, 128:] = total
        return unused

    lax.fori_loop(0, 16, slab_sum, 0)
    fold = pos_fold[...]
    for count in (64, 32, 16, 8):
        fold = fold[:count] + pltpu.roll(fold[count : 2 * count], 768 - count, 1)
    row_no = lax.broadcasted_iota(jnp.int32, (8, 768), 0)
    for count in (4, 2, 1):
        fold = jnp.where((row_no & count) != 0, pltpu.roll(fold, 768 - count, 1), fold)
    fold = pltpu.roll(fold, 767, 1)
    fold = jnp.broadcast_to(jnp.sum(fold, axis=0, keepdims=True), (8, 768))
    row8 = lax.broadcasted_iota(jnp.int32, (8, 128), 0)
    sums = jnp.zeros((8, 128), F32)
    for b in range(4):
        block = lanes_reversed(fold[:, (4 - b) * 128 : (5 - b) * 128])
        sums = jnp.where(row8 == b, block, sums)

    def histogram(first, blocks):
        def step(n, totals):
            i = first + lax.div(n, 16)
            rows = pl.ds(aligned(lax.rem(n, 16) * 8, 8), 8)
            grads = [bias[i, rows, 0:128] + bias[i, rows, 512:640]]
            numbers = [bucket[i, rows, 512:640]]
            for b in blocks:
                grads.append(bias[i, rows, b * 128 : b * 128 + 128])
                numbers.append(bucket[i, rows, b * 128 : b * 128 + 128])
            out = []
            for number in range(BUCKETS):
                part = totals[number]
                for at in range(len(grads)):
                    part = part + jnp.where(numbers[at] == number, grads[at], 0.0)
                out.append(part)
            return tuple(out)

        return step

    totals = tuple(jnp.zeros((8, 128), F32) for unused in range(BUCKETS))
    for first, count, blocks in ((0, 1, ()), (1, 1, (3,)), (2, 1, (2, 3)), (3, 1, (1, 2, 3))):
        totals = lax.fori_loop(0, 16 * count, histogram(first, blocks), totals)

    for k in range(1, NX):
        ax_copy(k).wait_recv()

    def a_sum(n, unused):
        to_yl = lax.div(n, 4)
        rows = pl.ds(aligned(lax.rem(n, 4) * 32, 32), 32)
        total = w_own[x, to_yl, rows, wide] + w_r0[x, to_yl, rows, wide].astype(F32)
        for k in range(1, NX):
            total = total + w_ax[k, to_yl, rows, :].astype(F32)
        w_a1[to_yl, rows, :] = total.astype(BF16)
        return unused

    lax.fori_loop(0, 8, a_sum, 0)
    for k in range(1, NZ):
        az_copy(k).start()
    for k in range(1, NZ):
        bz_copy(k).wait_recv()

    def b_sum(n, unused):
        total = w_own[n, :, z_rows(0), narrow_cols] + w_r0[n, :, z_rows(0), narrow_cols].astype(F32)
        for k in range(1, NZ):
            total = total + w_bz[k, n].astype(F32)
        w_b1[n] = total.astype(BF16)
        return unused

    lax.fori_loop(0, NX, b_sum, 0)
    for k in range(1, NX):
        bx_copy(k).start()

    totals = lax.fori_loop(0, 16 * 4, histogram(4, (1, 2, 3)), totals)
    lane8 = lax.broadcasted_iota(jnp.int32, (8, 128), 1)
    timed = jnp.zeros((8, 128), F32)
    for b in range(BUCKETS):
        whole = jnp.sum(jnp.sum(totals[b], axis=0, keepdims=True), axis=1, keepdims=True)
        timed = jnp.where(lane8 == b, whole, timed)
    sums = jnp.where(row8 == 4, timed, sums)

    slots = (z, x * NYL + yl, me)
    b_peers = (z_peer, xy_peer, ctx_peer)

    def b_copy(level, k):
        return remote(b_v.at[level], b_r.at[level, slots[level]], b_s.at[level, k], b_rs.at[level, k], b_peers[level](k))

    def b_start(level, value):
        b_v[level] = value
        b_r[level, slots[level]] = value
        for k in range(1, 8):
            b_copy(level, k).start()

    def b_finish(level):
        for k in range(1, 8):
            b_copy(level, k).wait_recv()
        value = b_r[level, 0]
        for slot in range(1, 8):
            value = value + b_r[level, slot]
        return value

    b_start(0, sums)

    def value_block(i):
        slab = pl.ds(aligned(i * ROWS), SLAB)
        d_send[2, i] = dot(wts_t[i + 4], doh[slab, :]).astype(BF16)

    def value_step(k, unused):
        value_block(lax.rem(me + k, CTX))
        d_copy(2, k).start()
        return unused

    lax.fori_loop(1, CTX, value_step, 0)
    value_block(me)

    d_own = [
        pltpu.make_async_copy(d_send.at[a, me], outs[a].at[0, :, my_cols], loc.at[8 + a])
        for a in range(3)
    ]
    for copy in d_own:
        copy.start()

    b_start(1, b_finish(0))

    y_slot = yl * NYH + yh

    def ry_copy(k):
        to_yl = lax.rem(yl + k // NYH, NYL)
        return remote(w_s2.at[to_yl], w_r3.at[y_slot], ry_s.at[k], ry_r.at[k], y_peer(k))

    for k in range(1, NZ):
        az_copy(k).wait_recv()
    total = w_a1[:, z_rows(0), :].astype(F32)
    for k in range(1, NZ):
        total = total + w_az[k].astype(F32)
    w_s2[:, :, wide] = total.astype(BF16)
    for k in range(1, NX):
        bx_copy(k).wait_recv()
    total = w_b1[x].astype(F32)
    for k in range(1, NX):
        total = total + w_bx[k].astype(F32)
    w_s2[:, :, narrow_cols] = total.astype(BF16)
    w_r3[y_slot] = w_s2[yl]
    for k in range(1, NYL * NYH):
        ry_copy(k).start()


    b_start(2, b_finish(1))

    for k in range(1, CTX):
        for a in range(3):
            qkv_copy(a, k).wait_send()
        for part in range(2):
            wz_copy(part, k).wait_send()
            o_copy(part, k).wait_send()
            a_copy(part, k).wait_send()
        bz_copy(k).wait_send()
    for k in range(1, NX):
        for which in range(2):
            wx_copy(which, k).wait_send()
        ax_copy(k).wait_send()
    for k in range(1, NX + 1):
        rc_copy(k).wait_send()
    for k in range(NX):
        wc_copy(k).wait_send()
    wy_copy().wait_send()

    for k in range(1, NYL * NYH):
        ry_copy(k).wait_recv()
    piece = w_r3[0].astype(F32)
    for slot in range(1, NYL * NYH):
        piece = piece + w_r3[slot].astype(F32)
    w_land[:, half] = piece

    def ag_copy():
        part = w_land.at[:, half]
        return remote(part, part, ag_s.at[0], ag_r.at[0], (dp, yh * 2 + 1 - core))

    ag_copy().start()


    ag_copy().wait_recv()
    wg_copy = pltpu.make_async_copy(w_land, wg_out, loc.at[15])
    wg_copy.start()

    sums = b_finish(2)
    table_v[0] = jnp.where(row8 < 4, sums, 0.0)
    table_v[1] = jnp.broadcast_to(sums[4:5, :], (8, 128))
    table_copies = [
        pltpu.make_async_copy(table_v.at[0], pos_out, loc.at[16]),
        pltpu.make_async_copy(table_v.at[1], time_out, loc.at[17]),
    ]
    for copy in table_copies:
        copy.start()

    for k in range(1, CTX):
        for a in range(3):
            b_copy(a, k).wait_send()
        az_copy(k).wait_send()
        ry_copy(k).wait_send()
    for k in range(1, NX):
        bx_copy(k).wait_send()
    ag_copy().wait_send()
    for copy in d_own + out_copies + table_copies + [wg_copy]:
        copy.wait()
    for a in (0, 1, 2):
        for k in range(1, CTX):
            d_copy(a, k).wait_recv()
            d_copy(a, k).wait_send()


def hand_over(*refs):
    given, results, held, sems = refs[:7], refs[8:15], refs[16:23], refs[23]
    reads = [pltpu.make_async_copy(given[n], held[n], sems.at[0, n]) for n in range(7)]
    writes = [pltpu.make_async_copy(held[n], results[n], sems.at[1, n]) for n in range(7)]
    for copy in reads:
        copy.start()
    refs[15][...] = refs[7][0, 0:32]
    for read, write in zip(reads, writes):
        read.wait()
        write.start()
    for copy in writes:
        copy.wait()


def on_device(
    query_in, key_in, value_in, gate_in, out_grad, out_weight, lengths, stamps, pos_bias, time_bias
):
    dma = lambda *shape: pltpu.SemaphoreType.DMA(shape)
    vmem = pltpu.VMEM
    anywhere = pl.BlockSpec(memory_space=pl.ANY)
    in_vmem = pl.BlockSpec(memory_space=pltpu.VMEM)
    rows_shape = jax.ShapeDtypeStruct((1, ROWS, COLS), BF16)
    outs = pl.pallas_call(
        kernel,
        out_shape=[rows_shape] * 5
        + [
            jax.ShapeDtypeStruct((WROWS, COLS), F32),
            jax.ShapeDtypeStruct((8, 128), F32),
            jax.ShapeDtypeStruct((8, 128), F32),
        ],
        in_specs=[anywhere] * 10,
        out_specs=[anywhere] * 8,
        scratch_shapes=[
            pltpu.SMEM((1, 8), jnp.int32),
            vmem((1, COLS), jnp.int32),
            vmem((8, 128), F32),
            pltpu.SMEM((32,), F32),
            vmem((2, 8, 128), F32),
            vmem((COLS, HEAD), BF16),
            vmem((PAD + COLS, HEAD), BF16),
            vmem((PAD + COLS, HEAD), BF16),
            vmem((COLS + PAD, HEAD), BF16),
            vmem((CTX, ROWS, HEAD), BF16),
            vmem((ROWS, COLS), BF16),
            vmem((ROWS, COLS), BF16),
            vmem((ROWS, COLS), BF16),
            vmem((ROWS, COLS), BF16),
            vmem((ROWS, COLS), BF16),
            vmem((ROWS, COLS), F32),
            vmem((NX, NYL, NZ * WROWS, COLS), BF16),
            vmem((1, PAD + COLS), jnp.int32),
            vmem((ROWS, SLAB), F32),
            vmem((CTX, ROWS, SLAB), F32),
            vmem((CTX, ROWS, SLAB), jnp.int32),
            vmem((CTX, ROWS, SLAB), BF16),
            vmem((CTX + 4, ROWS, SLAB), BF16),
            vmem((HEAD, COLS), BF16),
            vmem((HEAD, PAD + COLS), F32),
            vmem((3, CTX, ROWS, HEAD), BF16),
            vmem((ROWS, 768), F32),
            vmem((ROWS, COLS), BF16),
            vmem((ROWS, COLS), BF16),
            vmem((NX, NYL, 128, 512), BF16),
            vmem((NX, NYL, 128, 512), F32),
            vmem((NX, NYL, 128, 512), BF16),
            vmem((NX, NYL, 128, 512), BF16),
            vmem((NX, NYL, 128, 384), BF16),
            vmem((NYL, 128, 384), BF16),
            vmem((NZ, NYL, WROWS, 384), BF16),
            vmem((NZ, NX, NYL, WROWS, 128), BF16),
            vmem((NX, NYL, WROWS, 128), BF16),
            vmem((NX, NYL, WROWS, 128), BF16),
            vmem((NYL, WROWS, 512), BF16),
            vmem((NYL * NYH, WROWS, 512), BF16),
            vmem((WROWS, COLS), F32),
            vmem((3, 8, 128), F32),
            vmem((3, 8, 8, 128), F32),
            dma(18),
            dma(3, 8), dma(3, 8),
            dma(2, 8), dma(2, 8),
            dma(2, 4), dma(2, 4),
            dma(1), dma(1),
            dma(4), dma(4),
            dma(2, 8), dma(2, 8),
            dma(2, 8), dma(2, 8),
            dma(3, 8), dma(3, 8),
            dma(5), dma(5),
            dma(2, 4), dma(2, 4),
            dma(2, 8), dma(2, 8),
            dma(8), dma(8),
            dma(8), dma(8),
            dma(3, 8), dma(3, 8),
        ],
        compiler_params=pltpu.CompilerParams(
            collective_id=0, has_side_effects=True, vmem_limit_bytes=56 * 1024 * 1024
        ),
    )(
        query_in,
        key_in,
        value_in,
        gate_in,
        out_grad,
        out_weight,
        lengths,
        stamps,
        pos_bias.reshape(8, 128),
        time_bias,
    )
    outs = pl.pallas_call(
        hand_over,
        out_shape=[jax.ShapeDtypeStruct(out.shape, out.dtype) for out in outs[:7]]
        + [jax.ShapeDtypeStruct((32,), F32)],
        in_specs=[anywhere] * 7 + [in_vmem],
        out_specs=[anywhere] * 7 + [in_vmem],
        scratch_shapes=[vmem(out.shape, out.dtype) for out in outs[:7]] + [dma(2, 7)],
        compiler_params=pltpu.CompilerParams(vmem_limit_bytes=56 * 1024 * 1024),
    )(*outs)
    layer_out, query_grad, key_grad, value_grad, gate_grad, weight_grad, pos, timed = outs
    return (
        layer_out,
        query_grad,
        key_grad,
        value_grad,
        gate_grad,
        weight_grad,
        pos.reshape(COLS),
        timed,
    )


def solution(mesh):
    rows = P("dp", "ctx", None)
    owned = P("dp", None)
    return jax.shard_map(
        on_device,
        mesh=mesh,
        in_specs=(rows, rows, rows, rows, rows, owned, owned, owned, P(), P()),
        out_specs=(rows, rows, rows, rows, rows, owned, P(), P()),
        check_vma=False,
    )
```

```python
import functools

import jax
import jax.numpy as jnp
from jax import lax
from jax.experimental import pallas as pl
from jax.experimental.pallas import tpu as pltpu
from jax.sharding import PartitionSpec as P

HEAD = 128
ROWS = 128
CTX = 8
COLS = 1024
PAD = 512
SLAB = PAD + ROWS
NX, NYL, NZ, NYH = 4, 2, 8, 4
WROWS = 16
EPSILON = 1e-06
FACTOR = HEAD ** (-0.5)
MASKED = -1e30
BUCKETS = 24
F32 = jnp.float32
BF16 = jnp.bfloat16
NT = (((1,), (1,)), ((), ()))


def dot(a, b):
    return jnp.dot(a, b, preferred_element_type=F32)


def dot_nt(a, b):
    return lax.dot_general(a, b, NT, preferred_element_type=F32)


def aligned(start, size=128):
    return pl.multiple_of(start, size)


def lanes_reversed(block):
    lane = lax.broadcasted_iota(jnp.int32, block.shape, 1)
    return jnp.take_along_axis(block, 127 - lane, axis=1, mode="promise_in_bounds")


def gate_of(scores):
    return 0.5 * jnp.tanh(0.5 * scores) + 0.5


def kernel(
    q_in, k_in, v_in, g_in, og_in, w_in, len_in, stamp_in, pos_in, time_in,
    lo_out, dq_out, dk_out, dv_out, gg_out, wg_out, pos_out, time_out,
    len_ref, stamp_ref, pos_ref, time_ref, table_v,
    qh, kh, vh, doh, o_send, o_row, a_send, gate, ograd, mixed, mgrad, wbuf,
    stamp_pad, tz, bias, bucket, wts, wts_t, q_t, dk_t, d_send, pos_fold,
    lo_v, gg_v, w_send, w_own, w_r0, w_s0, w_ax, w_a1, w_az, w_bz, w_b1, w_bx, w_s2, w_r3, w_land,
    b_v, b_r,
    loc, qkv_s, qkv_r, wz_s, wz_r, wx_s, wx_r, wy_s, wy_r, wc_s, wc_r,
    o_s, o_r, a_s, a_r, d_s, d_r, rc_s, rc_r, rx_s, rx_r, rz_s, rz_r, ry_s, ry_r,
    ag_s, ag_r, b_s, b_rs,
):
    dp = lax.axis_index("dp")
    me = lax.axis_index("ctx")
    z = lax.rem(dp, NZ)
    yl = lax.rem(lax.div(dp, NZ), NYL)
    x = lax.div(dp, NZ * NYL)
    core = lax.rem(me, 2)
    yh = lax.div(me, 2)

    def dp_of(xx, yy, zz):
        return (xx * NYL + yy) * NZ + zz

    def ctx_peer(k):
        return (dp, lax.rem(me + k, CTX))

    def z_peer(k):
        return (dp_of(x, yl, lax.rem(z + k, NZ)), me)

    def x_peer(k):
        return (dp_of(lax.rem(x + k, NX), yl, z), me)

    def xy_peer(k):
        return (dp_of(lax.rem(x + k // 2, NX), lax.rem(yl + k % 2, NYL), z), me)

    def y_peer(k):
        return (dp_of(x, lax.rem(yl + k // NYH, NYL), z), lax.rem(yh + k % NYH, NYH) * 2 + core)

    def remote(src, dst, send_sem, recv_sem, where):
        return pltpu.make_async_remote_copy(
            src_ref=src,
            dst_ref=dst,
            send_sem=send_sem,
            recv_sem=recv_sem,
            device_id=where,
            device_id_type=pl.DeviceIdType.MESH,
        )

    partners = [ctx_peer(k) for k in range(1, CTX)]
    partners += [z_peer(k) for k in range(1, NZ)]
    partners += [xy_peer(k) for k in range(1, NX * NYL)]
    partners += [y_peer(NYH + k) for k in range(1, NYH)]
    barrier = pltpu.get_barrier_semaphore()
    for where in partners:
        pl.semaphore_signal(barrier, inc=1, device_id=where, device_id_type=pl.DeviceIdType.MESH)

    my_rows = pl.ds(aligned(me * ROWS), ROWS)
    my_pad_rows = pl.ds(aligned(PAD + me * ROWS), ROWS)
    my_cols = pl.ds(aligned(me * HEAD), HEAD)
    half = pl.ds(aligned(core * 512), 512)
    w_rows = pl.ds(aligned(z * WROWS, WROWS), WROWS)
    own_copies = [
        pltpu.make_async_copy(q_in.at[0, :, my_cols], qh.at[my_rows], loc.at[0]),
        pltpu.make_async_copy(k_in.at[0, :, my_cols], kh.at[my_pad_rows], loc.at[1]),
        pltpu.make_async_copy(v_in.at[0, :, my_cols], vh.at[my_pad_rows], loc.at[2]),
        pltpu.make_async_copy(g_in.at[0], gate, loc.at[3]),
        pltpu.make_async_copy(og_in.at[0], ograd, loc.at[4]),
        pltpu.make_async_copy(w_in.at[:, half], wbuf.at[x, yl, w_rows, half], loc.at[5]),
    ]
    small_copies = [
        pltpu.make_async_copy(len_in, len_ref, loc.at[11]),
        pltpu.make_async_copy(stamp_in, stamp_ref, loc.at[12]),
        pltpu.make_async_copy(pos_in, pos_ref, loc.at[13]),
        pltpu.make_async_copy(time_in, time_ref, loc.at[14]),
    ]
    for copy in small_copies:
        copy.start()
    pl.semaphore_wait(barrier, len(partners))

    def qkv_copy(a, k):
        where = ctx_peer(k)
        cols = pl.ds(aligned(where[1] * HEAD), HEAD)
        src = (q_in, k_in, v_in)[a].at[0, :, cols]
        dst = (qh.at[my_rows], kh.at[my_pad_rows], vh.at[my_pad_rows])[a]
        return remote(src, dst, qkv_s.at[a, k], qkv_r.at[a, k], where)

    def wy_copy():
        return remote(w_in.at[:, half], wbuf.at[x, yl, w_rows, half], wy_s.at[0], wy_r.at[0], (dp_of(x, 1 - yl, z), me))

    def wz_copy(which, k):
        dst = wbuf.at[x, yl if which == 0 else 1 - yl, w_rows, half]
        src = w_in.at[:, half] if which == 0 else dst
        return remote(src, dst, wz_s.at[which, k], wz_r.at[which, k], z_peer(k))

    def wx_copy(which, k):
        part = wbuf.at[x, yl if which == 0 else 1 - yl, :, half]
        return remote(part, part, wx_s.at[which, k], wx_r.at[which, k], x_peer(k))

    def wc_copy(k):
        part = wbuf.at[lax.rem(x + NX - k, NX), :, :, half]
        return remote(part, part, wc_s.at[k], wc_r.at[k], (dp, yh * 2 + 1 - core))

    wy_copy().start()
    for k in range(1, NZ):
        wz_copy(0, k).start()
    for k in (3, 4, 5, 2, 6, 1, 7):
        qkv_copy(0, k).start()
        qkv_copy(1, k).start()
    for copy in own_copies:
        copy.start()
    for k in (3, 4, 5, 2, 6, 1, 7):
        qkv_copy(2, k).start()
    kh[0:PAD, :] = jnp.zeros((PAD, HEAD), BF16)
    vh[0:PAD, :] = jnp.zeros((PAD, HEAD), BF16)
    doh[COLS:, :] = jnp.zeros((PAD, HEAD), BF16)
    for j in range(4, CTX):
        for t in range(CTX - j, 5):
            wts_t[j + 4, :, t * 128 : t * 128 + 128] = jnp.zeros((128, 128), BF16)
    dk_t[...] = jnp.zeros(dk_t.shape, F32)
    stamp_pad[:, 0:PAD] = jnp.zeros((1, PAD), jnp.int32)
    for copy in small_copies:
        copy.wait()
    stamp_pad[:, PAD:] = stamp_ref[...]

    reversed_pos = lanes_reversed(pos_ref[...])
    line = jnp.concatenate(
        [reversed_pos[4 - b : 5 - b, :] for b in range(5)] + [jnp.zeros((1, 128), F32)], axis=1
    )
    sheet = pltpu.roll(jnp.broadcast_to(line, (ROWS, 768)), 1, 1)
    row_no = lax.broadcasted_iota(jnp.int32, (ROWS, 768), 0)
    for bit in range(7):
        rolled = pltpu.roll(sheet, 1 << bit, 1)
        sheet = jnp.where((row_no & (1 << bit)) != 0, rolled, sheet)
    tz[...] = sheet[:, 128:]

    r_iota = lax.broadcasted_iota(jnp.int32, (ROWS, 128), 0)
    c_iota = lax.broadcasted_iota(jnp.int32, (ROWS, 128), 1)
    table = jnp.zeros((ROWS, 128), F32)
    for b in range(32):
        table = jnp.where(c_iota == b, time_ref[b], table)
    starts = []
    total = jnp.int32(0)
    for u in range(8):
        starts.append(total)
        total = total + len_ref[0, u]

    def bias_slab(i, unused):
        row_stamps = stamp_pad[:, pl.ds(aligned(PAD + i * ROWS), ROWS)]
        stamp_col = jnp.transpose(jnp.broadcast_to(row_stamps, (ROWS, 128)))
        place = r_iota + i * ROWS
        start = jnp.zeros((ROWS, 128), jnp.int32)
        for u in range(1, 8):
            start = jnp.where(place >= starts[u], jnp.maximum(start, starts[u]), start)
        first_col = start - (i * ROWS - PAD)
        numbers = []
        for b in range(5):
            key_stamps = stamp_pad[:, pl.ds(aligned(i * ROWS + b * 128), 128)]
            number = 32 - lax.clz(stamp_col - key_stamps)
            timed = jnp.take_along_axis(table, number, axis=1, mode="promise_in_bounds")
            col = c_iota + b * 128
            mask = (col >= first_col) & (col <= r_iota + PAD)
            cols = slice(b * 128, b * 128 + 128)
            bias[i, :, cols] = jnp.where(mask, tz[:, cols] + timed, MASKED)

            numbers.append(number)
            if b in (1, 2, 3):
                bucket[i, :, cols] = number
        bucket[i, :, 512:] = jnp.where(c_iota <= r_iota, numbers[4], numbers[0])
        return unused

    lax.fori_loop(0, CTX, bias_slab, 0)

    wy_copy().wait_recv()
    for k in range(1, NZ):
        wz_copy(1, k).start()
    own_copies[5].wait()
    for k in range(1, NZ):
        wz_copy(0, k).wait_recv()
    for k in range(1, NX):
        wx_copy(0, k).start()
    for k in range(1, NZ):
        wz_copy(1, k).wait_recv()
    for k in range(1, NX):
        wx_copy(1, k).start()
    wc_copy(0).start()

    for copy in own_copies[:5]:
        copy.wait()
    for a in (0, 1):
        for k in range(1, CTX):
            qkv_copy(a, k).wait_recv()

    def weigh(i, unused):
        rows = pl.ds(aligned(i * ROWS), ROWS)
        slab = pl.ds(aligned(i * ROWS), SLAB)
        pair_bias = bias[i]
        mask = pair_bias > 0.1 * MASKED
        scores = dot_nt(qh[rows, :], kh[slab, :]) * FACTOR + pair_bias
        sig = gate_of(scores)
        weights = jnp.where(mask, scores * sig, 0.0).astype(BF16)
        wts[i] = weights
        bias[i] = jnp.where(mask, sig * (1.0 + scores * (1.0 - sig)), 0.0)
        for b in range(5):
            turned = jnp.transpose(weights[:, b * 128 : b * 128 + 128])
            wts_t[i + b, :, (4 - b) * 128 : (5 - b) * 128] = turned
        q_t[:, rows] = jnp.transpose(qh[rows, :])
        return unused

    lax.fori_loop(0, CTX, weigh, 0)

    def attend(i):
        slab = pl.ds(aligned(i * ROWS), SLAB)
        return dot(wts[i], vh[slab, :]).astype(BF16)

    def part_rows(part):
        return pl.ds(part * 64, 64)

    def o_copy(part, k):
        where = ctx_peer(k)
        rows = part_rows(part)
        return remote(
            o_send.at[where[1], rows], o_row.at[rows, my_cols], o_s.at[part, k], o_r.at[part, k], where
        )

    def attend_step(k, unused):
        i = lax.rem(me + k, CTX)
        o_send[i] = attend(i)
        o_copy(0, k).start()
        return unused

    for k in range(1, CTX):
        qkv_copy(2, k).wait_recv()
    lax.fori_loop(1, CTX, attend_step, 0, unroll=7)
    for k in range(1, CTX):
        o_copy(1, k).start()
    o_row[:, my_cols] = attend(me)

    for k in range(1, NX):
        for which in range(2):
            wx_copy(which, k).wait_recv()
        wc_copy(k).start()
    for k in range(NX):
        wc_copy(k).wait_recv()

    def mixed_grad_part(n, unused):
        block = wbuf[n].reshape(256, COLS)
        mgrad[:, pl.ds(aligned(n * 256), 256)] = dot_nt(ograd[...], block)
        return unused

    lax.fori_loop(0, NX, mixed_grad_part, 0)

    def rows_part(n, unused):
        rows = pl.ds(aligned(n * 32, 32), 32)
        attended = o_row[rows, :].astype(F32)
        center = attended - jnp.mean(attended, axis=1, keepdims=True)
        inv_dev = lax.rsqrt(jnp.mean(center * center, axis=1, keepdims=True) + EPSILON)
        normed = center * inv_dev
        gate_wide = gate[rows, :].astype(F32)
        grad = mgrad[rows, :]
        mixed[rows, :] = (normed * gate_wide).astype(BF16)
        gg_v[rows, :] = (grad * normed).astype(BF16)
        normed_grad = grad * gate_wide
        first = jnp.mean(normed_grad, axis=1, keepdims=True)
        second = jnp.mean(normed_grad * normed, axis=1, keepdims=True)
        a_send[rows, :] = (inv_dev * (normed_grad - first - normed * second)).astype(BF16)
        return unused

    def a_copy(part, k):
        where = ctx_peer(k)
        cols = pl.ds(aligned(where[1] * HEAD), HEAD)
        rows = pl.ds(aligned(me * ROWS + part * 64, 64), 64)
        return remote(
            a_send.at[part_rows(part), cols], doh.at[rows], a_s.at[part, k], a_r.at[part, k], where
        )

    for part in range(2):
        for k in range(1, CTX):
            o_copy(part, k).wait_recv()
        lax.fori_loop(2 * part, 2 * part + 2, rows_part, 0)
        for k in range(1, CTX):
            a_copy(part, k).start()
    doh[my_rows, :] = a_send[:, my_cols]

    other_half = pl.ds(aligned((1 - core) * 512), 512)

    def rc_copy(k):
        part = lax.rem(x + k, NX)
        return remote(w_send.at[part], w_r0.at[part], rc_s.at[k], rc_r.at[k], (dp, yh * 2 + 1 - core))

    def weight_part(k, unused):
        part = lax.rem(x + k, NX)
        turned = jnp.transpose(mixed[:, pl.ds(aligned(part * 256), 256)])
        w_send[part] = dot(turned, ograd[:, other_half]).astype(BF16).reshape(2, 128, 512)
        rc_copy(k).start()
        w_own[part] = dot(turned, ograd[:, half]).reshape(2, 128, 512)
        return unused

    lax.fori_loop(1, NX + 1, weight_part, 0)

    wide, narrow_cols = pl.ds(0, 384), pl.ds(384, 128)

    def z_rows(k):
        return pl.ds(aligned(lax.rem(z + k, NZ) * WROWS, WROWS), WROWS)

    def ax_copy(k):
        part = lax.rem(x + k, NX)
        return remote(w_s0.at[part, :, :, wide], w_ax.at[k], rx_s.at[0, k], rx_r.at[0, k], x_peer(k))

    def az_copy(k):
        return remote(w_a1.at[:, z_rows(k)], w_az.at[k], rz_s.at[0, k], rz_r.at[0, k], z_peer(k))

    def bz_copy(k):
        src = w_s0.at[:, :, z_rows(k), narrow_cols]
        return remote(src, w_bz.at[k], rz_s.at[1, k], rz_r.at[1, k], z_peer(k))

    def bx_copy(k):
        part = lax.rem(x + k, NX)
        return remote(w_b1.at[part], w_bx.at[k], rx_s.at[1, k], rx_r.at[1, k], x_peer(k))

    def core_sum(k):
        part = lax.rem(x + k, NX)
        rc_copy(k).wait_recv()
        w_s0[part] = (w_own[part] + w_r0[part].astype(F32)).astype(BF16)

    def core_step(k, unused):
        core_sum(k)
        ax_copy(k).start()
        return unused

    lax.fori_loop(1, NX, core_step, 0)
    core_sum(NX)
    for k in range(1, NZ):
        bz_copy(k).start()

    def layer_part(n, unused):
        cols = pl.ds(aligned(n * 256), 256)
        block = wbuf[:, :, :, cols].reshape(COLS, 256)
        lo_v[:, cols] = dot(mixed[...], block).astype(BF16)
        return unused

    lax.fori_loop(0, 4, layer_part, 0)
    out_copies = [
        pltpu.make_async_copy(lo_v, lo_out.at[0], loc.at[6]),
        pltpu.make_async_copy(gg_v, gg_out.at[0], loc.at[7]),
    ]
    for copy in out_copies:
        copy.start()


    for part in range(2):
        for k in range(1, CTX):
            a_copy(part, k).wait_recv()

    outs = (dq_out, dk_out, dv_out)

    def d_copy(a, k):
        where = ctx_peer(k)
        return remote(d_send.at[a, where[1]], outs[a].at[0, :, my_cols], d_s.at[a, k], d_r.at[a, k], where)

    def query_block(i):
        rows = pl.ds(aligned(i * ROWS), ROWS)
        slab = pl.ds(aligned(i * ROWS), SLAB)
        score_grad = dot_nt(doh[rows, :], vh[slab, :]) * bias[i]
        bias[i] = score_grad
        narrow = score_grad.astype(BF16)
        dk_t[:, slab] += dot(q_t[:, rows], narrow)
        d_send[0, i] = (dot(narrow, kh[slab, :]) * FACTOR).astype(BF16)

    def query_step(k, unused):
        query_block(lax.rem(me + k, CTX))
        d_copy(0, k).start()
        return unused

    lax.fori_loop(1, CTX, query_step, 0, unroll=7)
    query_block(me)

    def key_block(i):
        rows = pl.ds(aligned(PAD + i * ROWS), ROWS)
        d_send[1, i] = (jnp.transpose(dk_t[:, rows]) * FACTOR).astype(BF16)

    def key_step(k, unused):
        key_block(lax.rem(me + k, CTX))
        d_copy(1, k).start()
        return unused

    lax.fori_loop(1, CTX, key_step, 0)
    key_block(me)
    pos_fold[:, 0:128] = jnp.zeros((ROWS, 128), F32)

    def slab_sum(n, unused):
        rows = pl.ds(aligned(n * 8, 8), 8)
        total = bias[0, rows, :]
        for i in range(1, CTX):
            total = total + bias[i, rows, :]
        pos_fold[rows, 128:] = total
        return unused

    lax.fori_loop(0, 16, slab_sum, 0)
    fold = pos_fold[...]
    for count in (64, 32, 16, 8):
        fold = fold[:count] + pltpu.roll(fold[count : 2 * count], 768 - count, 1)
    row_no = lax.broadcasted_iota(jnp.int32, (8, 768), 0)
    for count in (4, 2, 1):
        fold = jnp.where((row_no & count) != 0, pltpu.roll(fold, 768 - count, 1), fold)
    fold = pltpu.roll(fold, 767, 1)
    fold = jnp.broadcast_to(jnp.sum(fold, axis=0, keepdims=True), (8, 768))
    row8 = lax.broadcasted_iota(jnp.int32, (8, 128), 0)
    sums = jnp.zeros((8, 128), F32)
    for b in range(4):
        block = lanes_reversed(fold[:, (4 - b) * 128 : (5 - b) * 128])
        sums = jnp.where(row8 == b, block, sums)

    def histogram(first, blocks):
        def step(n, totals):
            i = first + lax.div(n, 16)
            rows = pl.ds(aligned(lax.rem(n, 16) * 8, 8), 8)
            grads = [bias[i, rows, 0:128] + bias[i, rows, 512:640]]
            numbers = [bucket[i, rows, 512:640]]
            for b in blocks:
                grads.append(bias[i, rows, b * 128 : b * 128 + 128])
                numbers.append(bucket[i, rows, b * 128 : b * 128 + 128])
            out = []
            for number in range(BUCKETS):
                part = totals[number]
                for at in range(len(grads)):
                    part = part + jnp.where(numbers[at] == number, grads[at], 0.0)
                out.append(part)
            return tuple(out)

        return step

    totals = tuple(jnp.zeros((8, 128), F32) for unused in range(BUCKETS))
    for first, count, blocks in ((0, 1, ()), (1, 1, (3,)), (2, 1, (2, 3)), (3, 1, (1, 2, 3))):
        totals = lax.fori_loop(0, 16 * count, histogram(first, blocks), totals)

    for k in range(1, NX):
        ax_copy(k).wait_recv()

    def a_sum(n, unused):
        to_yl = lax.div(n, 4)
        rows = pl.ds(aligned(lax.rem(n, 4) * 32, 32), 32)
        total = w_own[x, to_yl, rows, wide] + w_r0[x, to_yl, rows, wide].astype(F32)
        for k in range(1, NX):
            total = total + w_ax[k, to_yl, rows, :].astype(F32)
        w_a1[to_yl, rows, :] = total.astype(BF16)
        return unused

    lax.fori_loop(0, 8, a_sum, 0)
    for k in range(1, NZ):
        az_copy(k).start()
    for k in range(1, NZ):
        bz_copy(k).wait_recv()

    def b_sum(n, unused):
        total = w_own[n, :, z_rows(0), narrow_cols] + w_r0[n, :, z_rows(0), narrow_cols].astype(F32)
        for k in range(1, NZ):
            total = total + w_bz[k, n].astype(F32)
        w_b1[n] = total.astype(BF16)
        return unused

    lax.fori_loop(0, NX, b_sum, 0)
    for k in range(1, NX):
        bx_copy(k).start()

    totals = lax.fori_loop(0, 16 * 4, histogram(4, (1, 2, 3)), totals)
    lane8 = lax.broadcasted_iota(jnp.int32, (8, 128), 1)
    timed = jnp.zeros((8, 128), F32)
    for b in range(BUCKETS):
        whole = jnp.sum(jnp.sum(totals[b], axis=0, keepdims=True), axis=1, keepdims=True)
        timed = jnp.where(lane8 == b, whole, timed)
    sums = jnp.where(row8 == 4, timed, sums)

    slots = (z, x * NYL + yl, me)
    b_peers = (z_peer, xy_peer, ctx_peer)

    def b_copy(level, k):
        return remote(b_v.at[level], b_r.at[level, slots[level]], b_s.at[level, k], b_rs.at[level, k], b_peers[level](k))

    def b_start(level, value):
        b_v[level] = value
        b_r[level, slots[level]] = value
        for k in range(1, 8):
            b_copy(level, k).start()

    def b_finish(level):
        for k in range(1, 8):
            b_copy(level, k).wait_recv()
        value = b_r[level, 0]
        for slot in range(1, 8):
            value = value + b_r[level, slot]
        return value

    b_start(0, sums)

    def value_block(i):
        slab = pl.ds(aligned(i * ROWS), SLAB)
        d_send[2, i] = dot(wts_t[i + 4], doh[slab, :]).astype(BF16)

    def value_step(k, unused):
        value_block(lax.rem(me + k, CTX))
        d_copy(2, k).start()
        return unused

    lax.fori_loop(1, CTX, value_step, 0)
    value_block(me)

    d_own = [
        pltpu.make_async_copy(d_send.at[a, me], outs[a].at[0, :, my_cols], loc.at[8 + a])
        for a in range(3)
    ]
    for copy in d_own:
        copy.start()

    b_start(1, b_finish(0))

    y_slot = yl * NYH + yh

    def ry_copy(k):
        to_yl = lax.rem(yl + k // NYH, NYL)
        return remote(w_s2.at[to_yl], w_r3.at[y_slot], ry_s.at[k], ry_r.at[k], y_peer(k))

    for k in range(1, NZ):
        az_copy(k).wait_recv()
    total = w_a1[:, z_rows(0), :].astype(F32)
    for k in range(1, NZ):
        total = total + w_az[k].astype(F32)
    w_s2[:, :, wide] = total.astype(BF16)
    for k in range(1, NX):
        bx_copy(k).wait_recv()
    total = w_b1[x].astype(F32)
    for k in range(1, NX):
        total = total + w_bx[k].astype(F32)
    w_s2[:, :, narrow_cols] = total.astype(BF16)
    w_r3[y_slot] = w_s2[yl]
    for k in range(1, NYL * NYH):
        ry_copy(k).start()


    b_start(2, b_finish(1))

    for k in range(1, CTX):
        for a in range(3):
            qkv_copy(a, k).wait_send()
        for part in range(2):
            wz_copy(part, k).wait_send()
            o_copy(part, k).wait_send()
            a_copy(part, k).wait_send()
        bz_copy(k).wait_send()
    for k in range(1, NX):
        for which in range(2):
            wx_copy(which, k).wait_send()
        ax_copy(k).wait_send()
    for k in range(1, NX + 1):
        rc_copy(k).wait_send()
    for k in range(NX):
        wc_copy(k).wait_send()
    wy_copy().wait_send()

    for k in range(1, NYL * NYH):
        ry_copy(k).wait_recv()
    piece = w_r3[0].astype(F32)
    for slot in range(1, NYL * NYH):
        piece = piece + w_r3[slot].astype(F32)
    w_land[:, half] = piece

    def ag_copy():
        part = w_land.at[:, half]
        return remote(part, part, ag_s.at[0], ag_r.at[0], (dp, yh * 2 + 1 - core))

    ag_copy().start()


    ag_copy().wait_recv()
    wg_copy = pltpu.make_async_copy(w_land, wg_out, loc.at[15])
    wg_copy.start()

    sums = b_finish(2)
    table_v[0] = jnp.where(row8 < 4, sums, 0.0)
    table_v[1] = jnp.broadcast_to(sums[4:5, :], (8, 128))
    table_copies = [
        pltpu.make_async_copy(table_v.at[0], pos_out, loc.at[16]),
        pltpu.make_async_copy(table_v.at[1], time_out, loc.at[17]),
    ]
    for copy in table_copies:
        copy.start()

    for k in range(1, CTX):
        for a in range(3):
            b_copy(a, k).wait_send()
        az_copy(k).wait_send()
        ry_copy(k).wait_send()
    for k in range(1, NX):
        bx_copy(k).wait_send()
    ag_copy().wait_send()
    for copy in d_own + out_copies + table_copies + [wg_copy]:
        copy.wait()
    for a in (0, 1, 2):
        for k in range(1, CTX):
            d_copy(a, k).wait_recv()
            d_copy(a, k).wait_send()


def hand_over(*refs):
    given, results, held, sems = refs[:7], refs[8:15], refs[16:23], refs[23]
    reads = [pltpu.make_async_copy(given[n], held[n], sems.at[0, n]) for n in range(7)]
    writes = [pltpu.make_async_copy(held[n], results[n], sems.at[1, n]) for n in range(7)]
    for copy in reads:
        copy.start()
    refs[15][...] = refs[7][0, 0:32]
    for read, write in zip(reads, writes):
        read.wait()
        write.start()
    for copy in writes:
        copy.wait()


def on_device(
    query_in, key_in, value_in, gate_in, out_grad, out_weight, lengths, stamps, pos_bias, time_bias
):
    dma = lambda *shape: pltpu.SemaphoreType.DMA(shape)
    vmem = pltpu.VMEM
    anywhere = pl.BlockSpec(memory_space=pl.ANY)
    in_vmem = pl.BlockSpec(memory_space=pltpu.VMEM)
    rows_shape = jax.ShapeDtypeStruct((1, ROWS, COLS), BF16)
    outs = pl.pallas_call(
        kernel,
        out_shape=[rows_shape] * 5
        + [
            jax.ShapeDtypeStruct((WROWS, COLS), F32),
            jax.ShapeDtypeStruct((8, 128), F32),
            jax.ShapeDtypeStruct((8, 128), F32),
        ],
        in_specs=[anywhere] * 10,
        out_specs=[anywhere] * 8,
        scratch_shapes=[
            pltpu.SMEM((1, 8), jnp.int32),
            vmem((1, COLS), jnp.int32),
            vmem((8, 128), F32),
            pltpu.SMEM((32,), F32),
            vmem((2, 8, 128), F32),
            vmem((COLS, HEAD), BF16),
            vmem((PAD + COLS, HEAD), BF16),
            vmem((PAD + COLS, HEAD), BF16),
            vmem((COLS + PAD, HEAD), BF16),
            vmem((CTX, ROWS, HEAD), BF16),
            vmem((ROWS, COLS), BF16),
            vmem((ROWS, COLS), BF16),
            vmem((ROWS, COLS), BF16),
            vmem((ROWS, COLS), BF16),
            vmem((ROWS, COLS), BF16),
            vmem((ROWS, COLS), F32),
            vmem((NX, NYL, NZ * WROWS, COLS), BF16),
            vmem((1, PAD + COLS), jnp.int32),
            vmem((ROWS, SLAB), F32),
            vmem((CTX, ROWS, SLAB), F32),
            vmem((CTX, ROWS, SLAB), jnp.int32),
            vmem((CTX, ROWS, SLAB), BF16),
            vmem((CTX + 4, ROWS, SLAB), BF16),
            vmem((HEAD, COLS), BF16),
            vmem((HEAD, PAD + COLS), F32),
            vmem((3, CTX, ROWS, HEAD), BF16),
            vmem((ROWS, 768), F32),
            vmem((ROWS, COLS), BF16),
            vmem((ROWS, COLS), BF16),
            vmem((NX, NYL, 128, 512), BF16),
            vmem((NX, NYL, 128, 512), F32),
            vmem((NX, NYL, 128, 512), BF16),
            vmem((NX, NYL, 128, 512), BF16),
            vmem((NX, NYL, 128, 384), BF16),
            vmem((NYL, 128, 384), BF16),
            vmem((NZ, NYL, WROWS, 384), BF16),
            vmem((NZ, NX, NYL, WROWS, 128), BF16),
            vmem((NX, NYL, WROWS, 128), BF16),
            vmem((NX, NYL, WROWS, 128), BF16),
            vmem((NYL, WROWS, 512), BF16),
            vmem((NYL * NYH, WROWS, 512), BF16),
            vmem((WROWS, COLS), F32),
            vmem((3, 8, 128), F32),
            vmem((3, 8, 8, 128), F32),
            dma(18),
            dma(3, 8), dma(3, 8),
            dma(2, 8), dma(2, 8),
            dma(2, 4), dma(2, 4),
            dma(1), dma(1),
            dma(4), dma(4),
            dma(2, 8), dma(2, 8),
            dma(2, 8), dma(2, 8),
            dma(3, 8), dma(3, 8),
            dma(5), dma(5),
            dma(2, 4), dma(2, 4),
            dma(2, 8), dma(2, 8),
            dma(8), dma(8),
            dma(8), dma(8),
            dma(3, 8), dma(3, 8),
        ],
        compiler_params=pltpu.CompilerParams(
            collective_id=0, has_side_effects=True, vmem_limit_bytes=56 * 1024 * 1024
        ),
    )(
        query_in,
        key_in,
        value_in,
        gate_in,
        out_grad,
        out_weight,
        lengths,
        stamps,
        pos_bias.reshape(8, 128),
        time_bias,
    )
    outs = pl.pallas_call(
        hand_over,
        out_shape=[jax.ShapeDtypeStruct(out.shape, out.dtype) for out in outs[:7]]
        + [jax.ShapeDtypeStruct((32,), F32)],
        in_specs=[anywhere] * 7 + [in_vmem],
        out_specs=[anywhere] * 7 + [in_vmem],
        scratch_shapes=[vmem(out.shape, out.dtype) for out in outs[:7]] + [dma(2, 7)],
        compiler_params=pltpu.CompilerParams(vmem_limit_bytes=56 * 1024 * 1024),
    )(*outs)
    layer_out, query_grad, key_grad, value_grad, gate_grad, weight_grad, pos, timed = outs
    return (
        layer_out,
        query_grad,
        key_grad,
        value_grad,
        gate_grad,
        weight_grad,
        pos.reshape(COLS),
        timed,
    )


def solution(mesh):
    rows = P("dp", "ctx", None)
    owned = P("dp", None)
    return jax.shard_map(
        on_device,
        mesh=mesh,
        in_specs=(rows, rows, rows, rows, rows, owned, owned, owned, P(), P()),
        out_specs=(rows, rows, rows, rows, rows, owned, P(), P()),
        check_vma=False,
    )
```
